128 devices in a mesh: box: 64 (over y, x, z), dir: 2 (over core).
Axes of the slice: x: 4, y: 4, z: 4, core: 2. Of those that a mesh axis runs over, the one named last changes fastest.
Arguments:
- sources: bfloat16 [512, 2, 64, 512], P('box'), may hold values from -6 to 6
- near_blocks: bfloat16 [512, 3, 2, 512, 512], P('box', None, None, 'dir'), may hold values from -0.109375 to 0.109375
- near_src: int32 [512, 3], P('box'), may hold values from 0 to 511, as said below
- radiation: bfloat16 [512, 2, 512, 1024], P('box', None, None, 'dir'), may hold values from -0.1875 to 0.1875
- il0_src: int32 [512, 16], P('box'), may hold values from 0 to 511, as said below
- il0_rel: int32 [512, 16], P('box'), may hold values from 0 to 315
- il0_count: int32 [512], P('box'), may hold values from 1 to 16, as said below
- trans0: bfloat16 [316, 2, 1024], P(None, None, 'dir'), may hold values from -1 to 1
- phi_interp1: bfloat16 [64, 128], replicated, may hold values from -0.75 to 0.75
- theta_interp1: bfloat16 [32, 16], replicated, may hold values from -1.5 to 1.5
- shift1: bfloat16 [8, 2, 4096], replicated, may hold values from -1.5 to 1.5
- phi_interp2: bfloat16 [128, 256], replicated, may hold values from -0.5 to 0.5
- theta_interp2: bfloat16 [64, 32], replicated, may hold values from -1 to 1
- shift2: bfloat16 [8, 2, 16384], replicated, may hold values from -1.5 to 1.5
- il2_src: int32 [8, 4], replicated, may hold values from 0 to 7
- il2_rel: int32 [8, 4], replicated, may hold values from 0 to 315
- trans2: bfloat16 [316, 2, 64, 256], P(None, None, 'box', 'dir'), may hold values from -2 to 2
Outputs:
- near_field: float32 [512, 2, 64, 512], P('box', None, None, 'dir')
- leaf_incoming: float32 [512, 2, 64, 1024], P('box', None, None, 'dir')
- upper_incoming: float32 [8, 2, 64, 64, 256], P(None, None, None, 'box', 'dir')
The draws below stay inside these ranges and needn't reach their ends.
Inputs may be any that keep to these rules, and one draw needn't show every extreme that they name: `near_src`: every entry is a leaf box whose owner index (box // 8) differs from the owner index of the row's own box by at most one; the first entry of row b is b itself. `il0_src`: every entry is a leaf box whose owner index (box // 8) differs from the owner index of the row's own box by at most one. `il0_count`: among the 8 boxes of every owner, one has 16 valid entries.
All inputs are finite; a program needn't handle non-finite values.
Results may differ from the reference program's by a relative error of at most 0.012.
Values may be sent and summed in bfloat16 or wider, within the bound.
No kernel may reach another device: no remote copies, remote signals or barrier semaphores. Data moves between devices by JAX's collectives and lax.ppermute only.
A program may use at most 192 MiB of HBM per device.

```python
import jax
import jax.numpy as jnp
from jax import lax

P_SIZE = 512
NT0 = 16
NP0 = 64
NT1 = 32
NP1 = 128
NT2 = 64
NP2 = 256
BOX_DEV = 8
R = 64
NEAR = 3
IL0 = 16
NREL0 = 316
IL2 = 4
NREL2 = 316
OCT = 8
K0 = 1024
K1 = 4096
K2 = 16384
B0 = 512
B1 = 64
B2 = 8


def neighbour_boxes(key, count):
    step_key, slot_key = jax.random.split(key)
    owners_total = B0 // BOX_DEV
    owner = jnp.arange(B0, dtype=jnp.int32) // BOX_DEV
    offsets = jax.random.randint(step_key, (B0, count), -1, 2, dtype=jnp.int32)
    peers = jnp.clip(owner[:, None] + offsets, 0, owners_total - 1)
    slots = jax.random.randint(slot_key, (B0, count), 0, BOX_DEV, dtype=jnp.int32)
    return (peers * BOX_DEV + slots).astype(jnp.int32)


def draw_near_src(key, part):
    key = jax.random.fold_in(key, 11)
    links = neighbour_boxes(key, NEAR)
    return links.at[:, 0].set(jnp.arange(B0, dtype=jnp.int32))


def draw_il0_src(key, part):
    key = jax.random.fold_in(key, 12)
    links = neighbour_boxes(key, IL0)
    links = links.at[0, 0].set(0)
    return links.at[B0 - 1, 0].set(B0 - 1)


def draw_il0_count(key, part):
    key = jax.random.fold_in(key, 13)
    count_key, slot_key = jax.random.split(key)
    owners_total = B0 // BOX_DEV
    counts = jax.random.randint(count_key, (owners_total, BOX_DEV), 1, IL0 + 1, dtype=jnp.int32)
    chosen = jax.random.randint(slot_key, (owners_total, 1), 0, BOX_DEV, dtype=jnp.int32)
    positions = jnp.arange(BOX_DEV, dtype=jnp.int32)[None, :]
    counts = jnp.where(positions == chosen, IL0, counts)
    counts = jnp.where(positions == (chosen + 1) % BOX_DEV, 1, counts)
    return counts.reshape(B0).astype(jnp.int32)


def plant(array, own_key, low, largest):
    index_at = [jax.random.randint(jax.random.fold_in(own_key, axis), (), 0, length) for axis, length in enumerate(array.shape)]
    longest = array.shape.index(max(array.shape))
    beside = index_at[:longest] + [(index_at[longest] + 1) % array.shape[longest]] + index_at[longest + 1:]
    return array.at[tuple(index_at)].set(low).at[tuple(beside)].set(largest)


def level_of(rng, extent, cuts, low, top_value):
    def one(position, shards_of):
        steps = jax.random.uniform(jax.random.fold_in(jax.random.fold_in(rng, 6), position), (shards_of,), jnp.float32, low / len(cuts), top_value / len(cuts))
        return jnp.repeat(jnp.exp(steps), extent[position] // shards_of).reshape((-1,) + (1,) * (len(extent) - position - 1))

    loudness = one(*cuts[0])
    for cut in cuts[1:]:
        loudness = loudness * one(*cut)
    return loudness


def scatter_about(rng, extent, width, bound, cuts=(), kind=jnp.bfloat16):
    drawn = jax.random.normal(rng, extent, jnp.float32) * width
    if len(cuts) > 0:
        drawn = level_of(rng, extent, cuts, -0.22, 0.18) * drawn
    return jnp.clip(drawn, min=-bound, max=bound).astype(kind)


def setup_inputs(seed: int = 0) -> dict:
    arg_keys = jax.random.split(jax.random.key(seed), 18)
    sources = scatter_about(arg_keys[0], (B0, 2, R, P_SIZE), 1.0, 6.0, ((0, 64),))
    near_blocks = scatter_about(arg_keys[1], (B0, NEAR, 2, P_SIZE, P_SIZE), (2 * NEAR * P_SIZE) ** -0.5, 0.109375, ((0, 64), (3, 2)))
    near_src = draw_near_src(jax.random.fold_in(arg_keys[17], 71), 0)
    radiation = scatter_about(arg_keys[3], (B0, 2, P_SIZE, K0), (2 * P_SIZE) ** -0.5, 0.1875, ((0, 64), (3, 2)))
    il0_src = draw_il0_src(jax.random.fold_in(arg_keys[17], 71), 0)
    il0_rel = plant(jax.random.randint(arg_keys[5], (B0, IL0), 0, NREL0), jax.random.fold_in(arg_keys[5], 1), 0, NREL0 - 1).astype(jnp.int32)
    il0_count = draw_il0_count(jax.random.fold_in(arg_keys[17], 71), 0)
    trans0 = scatter_about(arg_keys[7], (NREL0, 2, K0), (2 * IL0) ** -0.5, 1.0, ((2, 2),))
    phi_interp1 = scatter_about(arg_keys[8], (NP0, NP1), NP0 ** -0.5, 0.75)
    theta_interp1 = scatter_about(arg_keys[9], (NT1, NT0), NT0 ** -0.5, 1.5)
    shift1 = scatter_about(arg_keys[10], (OCT, 2, K1), (2 * OCT) ** -0.5, 1.5)
    phi_interp2 = scatter_about(arg_keys[11], (NP1, NP2), NP1 ** -0.5, 0.5)
    theta_interp2 = scatter_about(arg_keys[12], (NT2, NT1), NT1 ** -0.5, 1.0)
    shift2 = scatter_about(arg_keys[13], (OCT, 2, K2), (2 * OCT) ** -0.5, 1.5)
    il2_src = plant(jax.random.randint(arg_keys[14], (B2, IL2), 0, B2), jax.random.fold_in(arg_keys[14], 1), 0, B2 - 1).astype(jnp.int32)
    il2_rel = plant(jax.random.randint(arg_keys[15], (B2, IL2), 0, NREL2), jax.random.fold_in(arg_keys[15], 1), 0, NREL2 - 1).astype(jnp.int32)
    trans2 = scatter_about(arg_keys[16], (NREL2, 2, NT2, NP2), (2 * IL2) ** -0.5, 2.0, ((2, 64), (3, 2)))
    return dict(sources=sources, near_blocks=near_blocks, near_src=near_src, radiation=radiation, il0_src=il0_src, il0_rel=il0_rel, il0_count=il0_count, trans0=trans0, phi_interp1=phi_interp1, theta_interp1=theta_interp1, shift1=shift1, phi_interp2=phi_interp2, theta_interp2=theta_interp2, shift2=shift2, il2_src=il2_src, il2_rel=il2_rel, trans2=trans2)


def pair_up(products):
    real_part = products[:, 0, 0] - products[:, 1, 1]
    imag_part = products[:, 0, 1] + products[:, 1, 0]
    return jnp.stack([real_part, imag_part], axis=1)


def translate(fetched, operators, weights):
    op_real = (operators[:, :, 0] * weights[:, :, None])[:, :, None, :]
    op_imag = (operators[:, :, 1] * weights[:, :, None])[:, :, None, :]
    real_part = jnp.sum(op_real * fetched[:, :, 0] - op_imag * fetched[:, :, 1], axis=1)
    imag_part = jnp.sum(op_real * fetched[:, :, 1] + op_imag * fetched[:, :, 0], axis=1)
    return jnp.stack([real_part, imag_part], axis=1)


def shifted_sum(values, factors):
    factor_real = factors[:, 0][:, None, :]
    factor_imag = factors[:, 1][:, None, :]
    real_part = jnp.sum(values[:, 0] * factor_real - values[:, 1] * factor_imag, axis=0)
    imag_part = jnp.sum(values[:, 0] * factor_imag + values[:, 1] * factor_real, axis=0)
    return jnp.stack([real_part, imag_part], axis=0)


def scale_pattern(values, factors):
    factor_real = factors[0][None, :]
    factor_imag = factors[1][None, :]
    real_part = values[0] * factor_real - values[1] * factor_imag
    imag_part = values[0] * factor_imag + values[1] * factor_real
    return jnp.stack([real_part, imag_part], axis=0)


def reference(sources, near_blocks, near_src, radiation, il0_src, il0_rel, il0_count, trans0, phi_interp1, theta_interp1, shift1, phi_interp2, theta_interp2, shift2, il2_src, il2_rel, trans2):
    groups = B0 // BOX_DEV
    group_ids = jnp.arange(groups, dtype=jnp.int32)

    def near_group(index):
        start = (index * BOX_DEV).astype(jnp.int32)
        blocks = lax.dynamic_slice_in_dim(near_blocks, start, BOX_DEV, 0).astype(jnp.float32)
        links = lax.dynamic_slice_in_dim(near_src, start, BOX_DEV, 0)
        picked = sources[links].astype(jnp.float32)
        return pair_up(jnp.einsum("bjcqp,bjerp->bcerq", blocks, picked))

    near_field = lax.map(near_group, group_ids).reshape(B0, 2, R, P_SIZE)

    def leaf_group(index):
        start = (index * BOX_DEV).astype(jnp.int32)
        rad_block = lax.dynamic_slice_in_dim(radiation, start, BOX_DEV, 0).astype(jnp.float32)
        src_block = lax.dynamic_slice_in_dim(sources, start, BOX_DEV, 0).astype(jnp.float32)
        return pair_up(jnp.einsum("berp,bcpk->bcerk", src_block, rad_block)).astype(jnp.bfloat16)

    leaf_out = lax.map(leaf_group, group_ids).reshape(B0, 2, R, K0)

    def translate_group(index):
        start = (index * BOX_DEV).astype(jnp.int32)
        links = lax.dynamic_slice_in_dim(il0_src, start, BOX_DEV, 0)
        kinds = lax.dynamic_slice_in_dim(il0_rel, start, BOX_DEV, 0)
        counts = lax.dynamic_slice_in_dim(il0_count, start, BOX_DEV, 0)
        fetched = leaf_out[links].astype(jnp.float32)
        operators = trans0[kinds].astype(jnp.float32)
        weights = (jnp.arange(IL0, dtype=jnp.int32)[None, :] < counts[:, None]).astype(jnp.float32)
        return translate(fetched, operators, weights)

    leaf_incoming = lax.map(translate_group, group_ids).reshape(B0, 2, R, K0)

    children = leaf_out.reshape(B1, OCT, 2, R, NT0, NP0)

    def parent_pattern(kids):
        along_phi = jnp.einsum("bcrtp,pq->bcrtq", kids.astype(jnp.float32), phi_interp1.astype(jnp.float32)).astype(jnp.bfloat16)
        along_phi = lax.optimization_barrier(along_phi)
        along_theta = jnp.einsum("st,bcrtq->bcrsq", theta_interp1.astype(jnp.float32), along_phi.astype(jnp.float32))
        along_theta = along_theta.reshape(OCT, 2, R, K1)
        return shifted_sum(along_theta, shift1.astype(jnp.float32)).astype(jnp.bfloat16)

    level_one = lax.map(parent_pattern, children)

    def upper_term(index):
        pattern = level_one[index].reshape(2, R, NT1, NP1)
        along_phi = jnp.einsum("crtp,pq->crtq", pattern.astype(jnp.float32), phi_interp2.astype(jnp.float32)).astype(jnp.bfloat16)
        along_phi = lax.optimization_barrier(along_phi)
        along_theta = jnp.einsum("st,crtq->crsq", theta_interp2.astype(jnp.float32), along_phi.astype(jnp.float32))
        along_theta = along_theta.reshape(2, R, K2)
        factors = shift2[index % OCT].astype(jnp.float32)
        return scale_pattern(along_theta, factors)

    terms = lax.map(upper_term, jnp.arange(B1, dtype=jnp.int32))
    level_two = jnp.sum(terms.reshape(B2, OCT, 2, R, K2), axis=1)
    upper_fetched = level_two[il2_src]
    upper_operators = trans2.reshape(NREL2, 2, K2)[il2_rel].astype(jnp.float32)
    upper_incoming = translate(upper_fetched, upper_operators, jnp.ones((B2, IL2), jnp.float32))
    return near_field, leaf_incoming, upper_incoming.reshape(B2, 2, R, NT2, NP2)
```

```python
import jax
import jax.numpy as jnp
from jax import lax
from jax.experimental import pallas as pl
from jax.experimental.pallas import tpu as pltpu
from jax.sharding import Mesh
from jax.sharding import PartitionSpec as P

BOX = ("y", "xh", "xl", "z")
ALL = BOX + ("dir",)
F32 = jnp.float32
BF16 = jnp.bfloat16
VMEM_LIMIT = 48 * 1024 * 1024


def params():
    return pltpu.CompilerParams(vmem_limit_bytes=VMEM_LIMIT)


def cost(flops, nbytes):
    return pl.CostEstimate(flops=flops, bytes_accessed=nbytes, transcendentals=0)


def dot(a, b):
    return lax.dot_general(a, b, (((1,), (0,)), ((), ())), preferred_element_type=F32)


def dot_nt(a, b):
    return lax.dot_general(a, b, (((1,), (1,)), ((), ())), preferred_element_type=F32)


def leaf_kernel(dir_ref, src_ref, rad_ref, leaf_ref, send_ref):
    rows = src_ref[0].reshape(128, 512)
    first = dot(rows, rad_ref[0, 0])
    second = dot(rows, rad_ref[0, 1])
    leaf_ref[0, 0] = (first[:64] - second[64:]).astype(BF16)
    leaf_ref[0, 1] = (second[:64] + first[64:]).astype(BF16)
    start = pl.multiple_of((1 - dir_ref[0]) * 32, 32)
    send_ref[0] = leaf_ref[0, :, pl.ds(start, 32), :]


def leaf_patterns(dir_index, sources, radiation):
    return pl.pallas_call(
        leaf_kernel,
        grid_spec=pltpu.PrefetchScalarGridSpec(
            num_scalar_prefetch=1,
            grid=(8,),
            in_specs=[
                pl.BlockSpec((1, 2, 64, 512), lambda b, d: (b, 0, 0, 0)),
                pl.BlockSpec((1, 2, 512, 512), lambda b, d: (b, 0, 0, 0)),
            ],
            out_specs=[
                pl.BlockSpec((1, 2, 64, 512), lambda b, d: (b, 0, 0, 0)),
                pl.BlockSpec((1, 2, 32, 512), lambda b, d: (b, 0, 0, 0)),
            ],
        ),
        out_shape=[
            jax.ShapeDtypeStruct((8, 2, 64, 512), BF16),
            jax.ShapeDtypeStruct((8, 2, 32, 512), BF16),
        ],
        compiler_params=params(),
        cost_estimate=cost(2 * 8 * 4 * 64 * 512 * 512, 11 << 20),
        name="leaf_patterns",
    )(dir_index, sources, radiation)


def level_one_kernel(
    dir_ref, mine_ref, other_ref, phi_ref, theta_ref, shift_ref, out_ref, expand, near, far, phi4, rows_f32
):
    step = pl.program_id(0)
    dir_index = dir_ref[0]

    @pl.when(step == 0)
    def _():
        spread = (
            lax.broadcasted_iota(jnp.int32, (32, 2048), 0)
            == lax.broadcasted_iota(jnp.int32, (32, 2048), 1) // 64
        ).astype(F32).astype(BF16)
        expand[...] = lax.dot_general(
            theta_ref[...], spread, (((0,), (0,)), ((), ())), preferred_element_type=F32
        )
        phi4[...] = jnp.zeros_like(phi4)
        for s in range(4):
            phi4[64 * s : 64 * s + 64, 128 * s : 128 * s + 128] = phi_ref[...]

    diagonal = (
        lax.broadcasted_iota(jnp.int32, (64, 256), 0) == lax.broadcasted_iota(jnp.int32, (64, 256), 1) % 64
    )
    near_rows = pl.multiple_of(dir_index * 8, 8)
    far_rows = pl.multiple_of((1 - dir_index) * 8, 8)
    for part in range(4):
        lanes = pl.ds(pl.multiple_of(step * 1024 + part * 256, 256), 256)
        near_values = expand[pl.ds(near_rows, 8), lanes]
        far_values = expand[pl.ds(far_rows, 8), lanes]
        for t in range(8):
            near[64 * t : 64 * t + 64, :] = jnp.where(diagonal, near_values[t : t + 1], 0.0).astype(BF16)
            far[64 * t : 64 * t + 64, :] = jnp.where(diagonal, far_values[t : t + 1], 0.0).astype(BF16)
        theta_out = dot(mine_ref[...].reshape(512, 512), near[...]) + dot(
            other_ref[...].reshape(512, 512), far[...]
        )
        fine = dot(theta_out.astype(BF16), phi4[...])
        real_sum = jnp.zeros((32, 512), F32)
        imag_sum = jnp.zeros((32, 512), F32)
        for b in range(8):
            real_part = fine[64 * b : 64 * b + 32]
            imag_part = fine[64 * b + 32 : 64 * b + 64]
            factors = shift_ref[b, :, 512 * part : 512 * part + 512].astype(F32)
            f_real, f_imag = factors[0:1], factors[1:2]
            real_sum = real_sum + (real_part * f_real - imag_part * f_imag)
            imag_sum = imag_sum + (real_part * f_imag + imag_part * f_real)
        for s in range(4):
            rows_f32[0:32, 4 * part + s, :] = real_sum[:, 128 * s : 128 * s + 128]
            rows_f32[32:64, 4 * part + s, :] = imag_sum[:, 128 * s : 128 * s + 128]
    for d in range(8):
        out_ref[d, 0] = rows_f32[4 * d : 4 * d + 4].astype(BF16)
        out_ref[d, 1] = rows_f32[32 + 4 * d : 36 + 4 * d].astype(BF16)


def level_one_patterns(dir_index, leaf, received, phi, theta, shift):
    return pl.pallas_call(
        level_one_kernel,
        grid_spec=pltpu.PrefetchScalarGridSpec(
            num_scalar_prefetch=1,
            grid=(2,),
            in_specs=[
                pl.BlockSpec((8, 2, 32, 512), lambda i, d: (0, 0, d[0], 0)),
                pl.BlockSpec((8, 2, 32, 512), lambda i, d: (0, 0, 0, 0)),
                pl.BlockSpec((64, 128), lambda i, d: (0, 0)),
                pl.BlockSpec((32, 16), lambda i, d: (0, 0)),
                pl.BlockSpec((8, 2, 2048), lambda i, d: (0, 0, i)),
            ],
            out_specs=pl.BlockSpec((8, 2, 4, 16, 128), lambda i, d: (0, 0, 0, i, 0)),
            scratch_shapes=[
                pltpu.VMEM((16, 2048), F32),
                pltpu.VMEM((512, 256), BF16),
                pltpu.VMEM((512, 256), BF16),
                pltpu.VMEM((256, 512), BF16),
                pltpu.VMEM((64, 16, 128), F32),
            ],
        ),
        out_shape=jax.ShapeDtypeStruct((8, 2, 4, 32, 128), BF16),
        compiler_params=params(),
        cost_estimate=cost(4 << 30, 2 << 20),
        name="level_one",
    )(dir_index, leaf, received, phi, theta, shift)


def level_two_kernel(kids_ref, phi_ref, theta_ref, shift_ref, out_ref, blocks, total, turned):
    tiled = dot(
        theta_ref[...],
        (
            lax.broadcasted_iota(jnp.int32, (32, 256), 0)
            == lax.broadcasted_iota(jnp.int32, (32, 256), 1) % 32
        ).astype(F32).astype(BF16),
    )
    owner = lax.broadcasted_iota(jnp.int32, (64, 256), 1) // 32
    for m in range(8):
        blocks[64 * m : 64 * m + 64, :] = jnp.where(owner == m, tiled, 0.0).astype(BF16)
    total[...] = jnp.zeros_like(total)

    def child(o, carry):
        along_phi = dot(kids_ref[o].reshape(256, 128), phi_ref[...]).astype(BF16)
        along_theta = dot(blocks[...], along_phi)
        f_real = shift_ref[o, 0].astype(F32)
        f_imag = shift_ref[o, 1].astype(F32)
        for r in range(4):
            real_part = along_theta[64 * r : 64 * r + 64]
            imag_part = along_theta[256 + 64 * r : 320 + 64 * r]
            total[r] = total[r] + (real_part * f_real - imag_part * f_imag)
            total[4 + r] = total[4 + r] + (real_part * f_imag + imag_part * f_real)
        return carry

    lax.fori_loop(0, 8, child, 0)
    for m in range(8):
        turned[:, m, :] = total[m]
    out_ref[:, 0] = turned[:, :, 0:128].astype(BF16)
    out_ref[:, 1] = turned[:, :, 128:256].astype(BF16)


def level_two_terms(kids, phi, theta, shift):
    return pl.pallas_call(
        level_two_kernel,
        out_shape=jax.ShapeDtypeStruct((64, 2, 8, 128), BF16),
        in_specs=[pl.BlockSpec(memory_space=pltpu.VMEM)] * 4,
        out_specs=pl.BlockSpec(memory_space=pltpu.VMEM),
        scratch_shapes=[
            pltpu.VMEM((512, 256), BF16),
            pltpu.VMEM((8, 64, 256), F32),
            pltpu.VMEM((64, 8, 256), F32),
        ],
        compiler_params=params(),
        cost_estimate=cost(2 << 30, 2 << 20),
        name="level_two",
    )(kids, phi, theta, shift)


def upper_kernel(src_ref, rel_ref, got_ref, ops_ref, out_ref, plain, rolled):
    for h in range(8):
        for g in range(8):
            for d in range(2):
                tile = got_ref[h, g, d].astype(F32)
                plain[h, 2 * g + d] = tile
                rolled[h, 2 * g + d] = pltpu.roll(tile, 4, 0)
    low = lax.broadcasted_iota(jnp.int32, (8, 128), 0) < 4

    def one(h, carry):
        total = jnp.zeros((16, 8, 128), F32)
        for i in range(4):
            operator = ops_ref[rel_ref[h, i]].astype(F32)
            op_real = jnp.broadcast_to(operator[0:1], (8, 128))
            op_imag = jnp.broadcast_to(operator[1:2], (8, 128))
            op_imag = jnp.where(low, -op_imag, op_imag)
            src = src_ref[h, i]
            total = total + (plain[src] * op_real[None] + rolled[src] * op_imag[None])
        for g in range(8):
            for d in range(2):
                start = 32 * d + 4 * g
                out_ref[h, 0, start : start + 4, :] = total[2 * g + d, 0:4]
                out_ref[h, 1, start : start + 4, :] = total[2 * g + d, 4:8]
        return carry

    lax.fori_loop(0, 8, one, 0)


def upper_translate(il2_src, il2_rel, got, operators):
    smem = pl.BlockSpec(memory_space=pltpu.SMEM)
    vmem = pl.BlockSpec(memory_space=pltpu.VMEM)
    return pl.pallas_call(
        upper_kernel,
        out_shape=jax.ShapeDtypeStruct((8, 2, 64, 128), F32),
        in_specs=[smem, smem, vmem, vmem],
        out_specs=vmem,
        scratch_shapes=[pltpu.VMEM((8, 16, 8, 128), F32), pltpu.VMEM((8, 16, 8, 128), F32)],
        compiler_params=params(),
        cost_estimate=cost(1 << 26, 1 << 20),
        name="upper_translate",
    )(il2_src, il2_rel, got, operators)


def near_kernel(
    link_ref, dir_ref, blocks_ref, own_ref, left_ref, left2_ref, right_ref, right2_ref, out_ref, boxes, sems
):
    b = pl.program_id(0)

    @pl.when(b == 0)
    def _():
        mine = pl.multiple_of(dir_ref[0] * 4, 4)
        theirs = pl.multiple_of((1 - dir_ref[0]) * 4, 4)
        copies = [
            pltpu.make_async_copy(own_ref, boxes.at[pl.ds(8, 8)], sems.at[0]),
            pltpu.make_async_copy(left_ref, boxes.at[pl.ds(mine, 4)], sems.at[1]),
            pltpu.make_async_copy(left2_ref, boxes.at[pl.ds(theirs, 4)], sems.at[2]),
            pltpu.make_async_copy(right_ref, boxes.at[pl.ds(16 + mine, 4)], sems.at[3]),
            pltpu.make_async_copy(right2_ref, boxes.at[pl.ds(16 + theirs, 4)], sems.at[4]),
        ]
        for copy in copies:
            copy.start()
        for copy in copies:
            copy.wait()

    first = jnp.zeros((128, 256), F32)
    second = jnp.zeros((128, 256), F32)
    for j in range(3):
        rows = boxes[link_ref[b, j]].reshape(128, 512)
        first = first + dot_nt(rows, blocks_ref[0, j, 0])
        second = second + dot_nt(rows, blocks_ref[0, j, 1])
    out_ref[0, 0] = first[:64] - second[64:]
    out_ref[0, 1] = second[:64] + first[64:]


def near_products(links, dir_index, near_blocks, own, left, left2, right, right2):
    anywhere = pl.BlockSpec(memory_space=pl.ANY)
    return pl.pallas_call(
        near_kernel,
        grid_spec=pltpu.PrefetchScalarGridSpec(
            num_scalar_prefetch=2,
            grid=(8,),
            in_specs=[pl.BlockSpec((1, 3, 2, 256, 512), lambda b, l, d: (b, 0, 0, 0, 0))] + [anywhere] * 5,
            out_specs=pl.BlockSpec((1, 2, 64, 256), lambda b, l, d: (b, 0, 0, 0)),
            scratch_shapes=[pltpu.VMEM((24, 2, 64, 512), BF16), pltpu.SemaphoreType.DMA((5,))],
        ),
        out_shape=jax.ShapeDtypeStruct((8, 2, 64, 256), F32),
        compiler_params=params(),
        cost_estimate=cost(2 * 24 * 4 * 64 * 256 * 512, 17 << 20),
        name="near_field",
    )(links, dir_index, near_blocks, own, left, left2, right, right2)


def translate_kernel(link_ref, rel_ref, count_ref, ops_ref, own_ref, left_ref, right_ref, out_ref, boxes, wide, sems):
    b = pl.program_id(0)

    @pl.when(b == 0)
    def _():
        copies = [
            pltpu.make_async_copy(left_ref, boxes.at[pl.ds(0, 8)], sems.at[0]),
            pltpu.make_async_copy(own_ref, boxes.at[pl.ds(8, 8)], sems.at[1]),
            pltpu.make_async_copy(right_ref, boxes.at[pl.ds(16, 8)], sems.at[2]),
        ]
        for copy in copies:
            copy.start()
        for copy in copies:
            copy.wait()

    count = count_ref[b]

    def widen(i, carry):
        wide[i] = ops_ref[rel_ref[b, i]].astype(F32)
        return carry

    lax.fori_loop(0, count, widen, 0)
    for chunk in range(4):
        rows = slice(16 * chunk, 16 * chunk + 16)

        def one(i, carry):
            real_sum, imag_sum = carry
            link = link_ref[b, i]
            real_part = boxes[link, 0, rows, :].astype(F32)
            imag_part = boxes[link, 1, rows, :].astype(F32)
            op_real = wide[i, 0:1, :]
            op_imag = wide[i, 1:2, :]
            real_sum = real_sum + (op_real * real_part - op_imag * imag_part)
            imag_sum = imag_sum + (op_real * imag_part + op_imag * real_part)
            return real_sum, imag_sum

        zero = jnp.zeros((16, 512), F32)
        real_sum, imag_sum = lax.fori_loop(0, count, one, (zero, zero))
        out_ref[0, 0, rows, :] = real_sum
        out_ref[0, 1, rows, :] = imag_sum


def leaf_translate(links, rel, count, operators, own, left, right):
    anywhere = pl.BlockSpec(memory_space=pl.ANY)
    return pl.pallas_call(
        translate_kernel,
        grid_spec=pltpu.PrefetchScalarGridSpec(
            num_scalar_prefetch=3,
            grid=(8,),
            in_specs=[pl.BlockSpec((316, 2, 512), lambda b, l, r, c: (0, 0, 0))] + [anywhere] * 3,
            out_specs=pl.BlockSpec((1, 2, 64, 512), lambda b, l, r, c: (b, 0, 0, 0)),
            scratch_shapes=[
                pltpu.VMEM((24, 2, 64, 512), BF16),
                pltpu.VMEM((16, 2, 512), F32),
                pltpu.SemaphoreType.DMA((3,)),
            ],
        ),
        out_shape=jax.ShapeDtypeStruct((8, 2, 64, 512), F32),
        compiler_params=params(),
        cost_estimate=cost(1 << 30, 6 << 20),
        name="leaf_translate",
    )(links, rel, count, operators, own, left, right)


def local(
    sources,
    near_blocks,
    near_src,
    radiation,
    il0_src,
    il0_rel,
    il0_count,
    trans0,
    phi_interp1,
    theta_interp1,
    shift1,
    phi_interp2,
    theta_interp2,
    shift2,
    il2_src,
    il2_rel,
    trans2,
):
    box_index = lax.axis_index(BOX)
    dir_position = lax.axis_index("dir")
    dir_index = dir_position.astype(jnp.int32).reshape(1)
    owners = lax.axis_size(BOX)
    first_box = (box_index - 1) * 8
    to_right = [(i, (i + 1) % owners) for i in range(owners)]
    to_left = [((i + 1) % owners, i) for i in range(owners)]
    swap = [(0, 1), (1, 0)]

    half = lax.dynamic_slice_in_dim(sources, dir_position * 4, 4, 0)
    left = lax.ppermute(half, BOX, to_right)
    right = lax.ppermute(half, BOX, to_left)
    left2 = lax.ppermute(left, "dir", swap)
    right2 = lax.ppermute(right, "dir", swap)

    leaf, send = leaf_patterns(dir_index, sources, radiation)
    leaf_left = lax.ppermute(leaf, BOX, to_right)
    leaf_right = lax.ppermute(leaf, BOX, to_left)
    received = lax.ppermute(send, "dir", swap)

    level_one = level_one_patterns(dir_index, leaf, received, phi_interp1, theta_interp1, shift1)
    kids = lax.all_to_all(level_one, ("xl", "z"), 0, 0, tiled=True)
    terms = level_two_terms(kids, phi_interp2, theta_interp2, shift2.reshape(8, 2, 64, 256))
    got = lax.all_to_all(terms.reshape(128, 8, 128), ALL, 0, 0, tiled=True)

    near_field = near_products(
        (near_src - first_box).astype(jnp.int32), dir_index, near_blocks, sources, left, left2, right, right2
    )
    leaf_incoming = leaf_translate(
        (il0_src - first_box).astype(jnp.int32), il0_rel, il0_count, trans0, leaf, leaf_left, leaf_right
    )
    upper = upper_translate(il2_src, il2_rel, got.reshape(8, 8, 2, 8, 128), trans2.reshape(316, 2, 128))
    return near_field, leaf_incoming, upper.reshape(8, 2, 64, 1, 128)


def solution(mesh):
    fine = Mesh(mesh.devices.reshape(4, 2, 2, 4, 2), ALL)
    placed = (
        P(BOX, None, None, None),
        P(BOX, None, None, "dir", None),
        P(BOX, None),
        P(BOX, None, None, "dir"),
        P(BOX, None),
        P(BOX, None),
        P(BOX),
        P(None, None, "dir"),
        P(),
        P(),
        P(),
        P(),
        P(),
        P(),
        P(),
        P(),
        P(None, None, BOX, "dir"),
    )
    return jax.shard_map(
        local,
        mesh=fine,
        in_specs=placed,
        out_specs=(
            P(BOX, None, None, "dir"),
            P(BOX, None, None, "dir"),
            P(None, None, None, BOX, "dir"),
        ),
        check_vma=False,
    )
```

```python
import functools

import jax
import jax.numpy as jnp
from jax import lax
from jax.experimental import pallas as pl
from jax.experimental.pallas import tpu as pltpu
from jax.sharding import Mesh
from jax.sharding import PartitionSpec as P

BOX = ("y", "xh", "xl", "z")
ALL = BOX + ("dir",)
F32 = jnp.float32
BF16 = jnp.bfloat16
HBM = pl.BlockSpec(memory_space=pltpu.HBM)
VMEM = pl.BlockSpec(memory_space=pltpu.VMEM)
SMEM = pl.BlockSpec(memory_space=pltpu.SMEM)
ANYWHERE = pl.BlockSpec(memory_space=pl.ANY)


def params(mebibytes):
    return pltpu.CompilerParams(vmem_limit_bytes=mebibytes << 20)


def cost(flops, nbytes):
    return pl.CostEstimate(flops=flops, bytes_accessed=nbytes, transcendentals=0)


def in_hbm(x):
    return pltpu.with_memory_space_constraint(x, pltpu.HBM)


def dot(a, b):
    return lax.dot_general(a, b, (((1,), (0,)), ((), ())), preferred_element_type=F32)


def dot_nt(a, b):
    return lax.dot_general(a, b, (((1,), (1,)), ((), ())), preferred_element_type=F32)


def leaf_kernel(
    dir_ref,
    src_hbm,
    rad_hbm,
    half_hbm,
    send_hbm,
    low_ref,
    high_ref,
    mine_ref,
    src,
    rad,
    leaf,
    src_sem,
    half_sem,
    rad_sems,
    send_sems,
):
    src_copy = pltpu.make_async_copy(src_hbm, src, src_sem)
    src_copy.start()
    for b in range(8):
        pltpu.make_async_copy(rad_hbm.at[b], rad.at[b], rad_sems.at[b]).start()
    src_copy.wait()
    first_box = pl.multiple_of(dir_ref[0] * 4, 4)
    half_copy = pltpu.make_async_copy(src.at[pl.ds(first_box, 4)], half_hbm, half_sem)
    half_copy.start()
    mine = pl.multiple_of(dir_ref[0] * 32, 32)
    other = pl.multiple_of((1 - dir_ref[0]) * 32, 32)

    def send(b):
        return pltpu.make_async_copy(leaf.at[b, :, pl.ds(other, 32), :], send_hbm.at[b], send_sems.at[b])

    def box(b, carry):
        pltpu.make_async_copy(rad_hbm.at[b], rad.at[b], rad_sems.at[b]).wait()
        rows = src[b].reshape(128, 512)
        first = dot(rows, rad[b, 0])
        second = dot(rows, rad[b, 1])
        leaf[b, 0] = (first[:64] - second[64:]).astype(BF16)
        leaf[b, 1] = (second[:64] + first[64:]).astype(BF16)
        send(b).start()
        low_ref[b] = leaf[b, :, :32, :]
        high_ref[b] = leaf[b, :, 32:, :]
        mine_ref[b] = leaf[b, :, pl.ds(mine, 32), :]
        return carry

    lax.fori_loop(0, 8, box, 0)
    half_copy.wait()
    for b in range(8):
        send(b).wait()


def leaf_patterns(dir_index, sources, radiation):
    return pl.pallas_call(
        leaf_kernel,
        in_specs=[SMEM, HBM, HBM],
        out_specs=[HBM, HBM, VMEM, VMEM, VMEM],
        out_shape=[jax.ShapeDtypeStruct((4, 2, 64, 512), BF16)]
        + [jax.ShapeDtypeStruct((8, 2, 32, 512), BF16)] * 4,
        scratch_shapes=[
            pltpu.VMEM((8, 2, 64, 512), BF16),
            pltpu.VMEM((8, 2, 512, 512), BF16),
            pltpu.VMEM((8, 2, 64, 512), BF16),
            pltpu.SemaphoreType.DMA,
            pltpu.SemaphoreType.DMA,
            pltpu.SemaphoreType.DMA((8,)),
            pltpu.SemaphoreType.DMA((8,)),
        ],
        compiler_params=params(16),
        cost_estimate=cost(1, 1),
        name="leaf_patterns",
    )(dir_index, in_hbm(sources), in_hbm(radiation))


def level_one_kernel(
    dir_ref, mine_ref, other_ref, phi_ref, theta_ref, shift_ref, out_ref, expand, near, far, phi4, rows_f32
):
    step = pl.program_id(0)
    dir_index = dir_ref[0]

    @pl.when(step == 0)
    def _():
        spread = (
            lax.broadcasted_iota(jnp.int32, (32, 2048), 0)
            == lax.broadcasted_iota(jnp.int32, (32, 2048), 1) // 64
        ).astype(F32).astype(BF16)
        expand[...] = lax.dot_general(
            theta_ref[...], spread, (((0,), (0,)), ((), ())), preferred_element_type=F32
        )
        phi4[...] = jnp.zeros_like(phi4)
        for s in range(4):
            phi4[64 * s : 64 * s + 64, 128 * s : 128 * s + 128] = phi_ref[...]

    diagonal = (
        lax.broadcasted_iota(jnp.int32, (64, 256), 0) == lax.broadcasted_iota(jnp.int32, (64, 256), 1) % 64
    )
    near_rows = pl.multiple_of(dir_index * 8, 8)
    far_rows = pl.multiple_of((1 - dir_index) * 8, 8)
    for part in range(4):
        lanes = pl.ds(pl.multiple_of(step * 1024 + part * 256, 256), 256)
        near_values = expand[pl.ds(near_rows, 8), lanes]
        far_values = expand[pl.ds(far_rows, 8), lanes]
        for t in range(8):
            near[64 * t : 64 * t + 64, :] = jnp.where(diagonal, near_values[t : t + 1], 0.0).astype(BF16)
            far[64 * t : 64 * t + 64, :] = jnp.where(diagonal, far_values[t : t + 1], 0.0).astype(BF16)
        theta_out = dot(mine_ref[...].reshape(512, 512), near[...]) + dot(
            other_ref[...].reshape(512, 512), far[...]
        )
        fine = dot(theta_out.astype(BF16), phi4[...])
        real_sum = jnp.zeros((32, 512), F32)
        imag_sum = jnp.zeros((32, 512), F32)
        for b in range(8):
            real_part = fine[64 * b : 64 * b + 32]
            imag_part = fine[64 * b + 32 : 64 * b + 64]
            factors = shift_ref[b, :, 512 * part : 512 * part + 512].astype(F32)
            f_real, f_imag = factors[0:1], factors[1:2]
            real_sum = real_sum + (real_part * f_real - imag_part * f_imag)
            imag_sum = imag_sum + (real_part * f_imag + imag_part * f_real)
        for s in range(4):
            rows_f32[0:32, 4 * part + s, :] = real_sum[:, 128 * s : 128 * s + 128]
            rows_f32[32:64, 4 * part + s, :] = imag_sum[:, 128 * s : 128 * s + 128]
    for d in range(8):
        out_ref[d, 0] = rows_f32[4 * d : 4 * d + 4].astype(BF16)
        out_ref[d, 1] = rows_f32[32 + 4 * d : 36 + 4 * d].astype(BF16)


def level_one_patterns(dir_index, leaf, received, phi, theta, shift):
    return pl.pallas_call(
        level_one_kernel,
        grid_spec=pltpu.PrefetchScalarGridSpec(
            num_scalar_prefetch=1,
            grid=(2,),
            in_specs=[
                pl.BlockSpec((8, 2, 32, 512), lambda i, d: (0, 0, 0, 0)),
                pl.BlockSpec((8, 2, 32, 512), lambda i, d: (0, 0, 0, 0)),
                pl.BlockSpec((64, 128), lambda i, d: (0, 0)),
                pl.BlockSpec((32, 16), lambda i, d: (0, 0)),
                pl.BlockSpec((8, 2, 2048), lambda i, d: (0, 0, i)),
            ],
            out_specs=pl.BlockSpec((8, 2, 4, 16, 128), lambda i, d: (0, 0, 0, i, 0)),
            scratch_shapes=[
                pltpu.VMEM((16, 2048), F32),
                pltpu.VMEM((512, 256), BF16),
                pltpu.VMEM((512, 256), BF16),
                pltpu.VMEM((256, 512), BF16),
                pltpu.VMEM((64, 16, 128), F32),
            ],
        ),
        out_shape=jax.ShapeDtypeStruct((8, 2, 4, 32, 128), BF16),
        compiler_params=params(24),
        cost_estimate=cost(1, 1),
        name="level_one",
    )(dir_index, leaf, received, phi, theta, shift)


def level_two_kernel(kids_ref, phi_ref, theta_ref, shift_ref, out_ref, blocks, total, turned):
    tiled = dot(
        theta_ref[...],
        (
            lax.broadcasted_iota(jnp.int32, (32, 256), 0)
            == lax.broadcasted_iota(jnp.int32, (32, 256), 1) % 32
        ).astype(F32).astype(BF16),
    )
    owner = lax.broadcasted_iota(jnp.int32, (64, 256), 1) // 32
    for m in range(8):
        blocks[64 * m : 64 * m + 64, :] = jnp.where(owner == m, tiled, 0.0).astype(BF16)
    total[...] = jnp.zeros_like(total)

    def child(o, carry):
        along_phi = dot(kids_ref[o].reshape(256, 128), phi_ref[...]).astype(BF16)
        along_theta = dot(blocks[...], along_phi)
        f_real = shift_ref[o, 0].astype(F32)
        f_imag = shift_ref[o, 1].astype(F32)
        for r in range(4):
            real_part = along_theta[64 * r : 64 * r + 64]
            imag_part = along_theta[256 + 64 * r : 320 + 64 * r]
            total[r] = total[r] + (real_part * f_real - imag_part * f_imag)
            total[4 + r] = total[4 + r] + (real_part * f_imag + imag_part * f_real)
        return carry

    lax.fori_loop(0, 8, child, 0)
    for m in range(8):
        turned[:, m, :] = total[m]
    out_ref[:, 0] = turned[:, :, 0:128].astype(BF16)
    out_ref[:, 1] = turned[:, :, 128:256].astype(BF16)


def level_two_terms(kids, phi, theta, shift):
    return pl.pallas_call(
        level_two_kernel,
        out_shape=jax.ShapeDtypeStruct((64, 2, 8, 128), BF16),
        in_specs=[pl.BlockSpec(memory_space=pltpu.VMEM)] * 4,
        out_specs=pl.BlockSpec(memory_space=pltpu.VMEM),
        scratch_shapes=[
            pltpu.VMEM((512, 256), BF16),
            pltpu.VMEM((8, 64, 256), F32),
            pltpu.VMEM((64, 8, 256), F32),
        ],
        compiler_params=params(16),
        cost_estimate=cost(1, 1),
        name="level_two",
    )(kids, phi, theta, shift)


def upper_operators_kernel(rel_ref, ops_ref, after_ref, out_ref):
    del after_ref
    for h in range(8):
        for i in range(4):
            out_ref[h, i] = ops_ref[rel_ref[h, i]].astype(F32)


def upper_operators(rel, operators, after):
    return pl.pallas_call(
        upper_operators_kernel,
        in_specs=[SMEM, VMEM, ANYWHERE],
        out_specs=VMEM,
        out_shape=jax.ShapeDtypeStruct((8, 4, 2, 128), F32),
        compiler_params=params(8),
        cost_estimate=cost(1 << 34, 1),
        name="upper_operators",
    )(rel, operators, after)


def upper_kernel(src_ref, got_ref, ops_ref, out_ref, plain, rolled):
    for h in range(8):
        for g in range(8):
            for d in range(2):
                tile = got_ref[h, g, d].astype(F32)
                plain[h, 2 * g + d] = tile
                rolled[h, 2 * g + d] = pltpu.roll(tile, 4, 0)
    low = lax.broadcasted_iota(jnp.int32, (8, 128), 0) < 4

    def one(h, carry):
        total = jnp.zeros((16, 8, 128), F32)
        for i in range(4):
            operator = ops_ref[h, i]
            op_real = jnp.broadcast_to(operator[0:1], (8, 128))
            op_imag = jnp.broadcast_to(operator[1:2], (8, 128))
            op_imag = jnp.where(low, -op_imag, op_imag)
            src = src_ref[h, i]
            total = total + (plain[src] * op_real[None] + rolled[src] * op_imag[None])
        for g in range(8):
            for d in range(2):
                start = 32 * d + 4 * g
                out_ref[h, 0, start : start + 4, :] = total[2 * g + d, 0:4]
                out_ref[h, 1, start : start + 4, :] = total[2 * g + d, 4:8]
        return carry

    lax.fori_loop(0, 8, one, 0)


def upper_translate(il2_src, got, operators):
    return pl.pallas_call(
        upper_kernel,
        out_shape=jax.ShapeDtypeStruct((8, 2, 64, 128), F32),
        in_specs=[SMEM, VMEM, VMEM],
        out_specs=VMEM,
        scratch_shapes=[pltpu.VMEM((8, 16, 8, 128), F32), pltpu.VMEM((8, 16, 8, 128), F32)],
        compiler_params=params(12),
        cost_estimate=cost(1 << 34, 1),
        name="upper_translate",
    )(il2_src, got, operators)


def near_kernel(
    link_ref,
    place_ref,
    blocks_hbm,
    own_hbm,
    one_hbm,
    one2_hbm,
    two_hbm,
    two2_hbm,
    out_hbm,
    blocks,
    boxes,
    result,
    self_sems,
    block_sems,
    box_sems,
    out_sems,
):
    mine = place_ref[0] * 4
    theirs = 4 - mine
    one = place_ref[1] * 16
    two = 16 - one

    def beside(source, start, sem):
        return pltpu.make_async_copy(source, boxes.at[pl.ds(pl.multiple_of(start, 4), 4)], box_sems.at[sem])

    def self_block(b):
        return pltpu.make_async_copy(blocks_hbm.at[b, 0], blocks.at[b, 0], self_sems.at[b])

    def other_blocks(b):
        rest = pl.ds(1, 2)
        return pltpu.make_async_copy(blocks_hbm.at[b, rest], blocks.at[b, rest], block_sems.at[b])

    own_copy = pltpu.make_async_copy(own_hbm, boxes.at[pl.ds(8, 8)], box_sems.at[4])
    own_copy.start()
    for b in range(8):
        self_block(b).start()
    copies = [
        beside(one_hbm, one + mine, 0),
        beside(one2_hbm, one + theirs, 1),
        beside(two_hbm, two + mine, 2),
        beside(two2_hbm, two + theirs, 3),
    ]
    for copy in copies:
        copy.start()
    for b in range(8):
        other_blocks(b).start()

    def product(b, j, box):
        rows = boxes[box].reshape(128, 512)
        first = dot_nt(rows, blocks[b, j, 0])
        second = dot_nt(rows, blocks[b, j, 1])
        return first[:64] - second[64:], second[:64] + first[64:]

    own_copy.wait()

    def itself(b, carry):
        self_block(b).wait()
        result[b, 0], result[b, 1] = product(b, 0, link_ref[b, 0])
        return carry

    lax.fori_loop(0, 8, itself, 0)
    for copy in copies:
        copy.wait()

    def others(b, carry):
        other_blocks(b).wait()
        real_one, imag_one = product(b, 1, link_ref[b, 1])
        real_two, imag_two = product(b, 2, link_ref[b, 2])
        result[b, 0] = result[b, 0] + (real_one + real_two)
        result[b, 1] = result[b, 1] + (imag_one + imag_two)
        pltpu.make_async_copy(result.at[b], out_hbm.at[b], out_sems.at[b]).start()
        return carry

    lax.fori_loop(0, 8, others, 0)
    for b in range(8):
        pltpu.make_async_copy(result.at[b], out_hbm.at[b], out_sems.at[b]).wait()


def near_products(links, places, near_blocks, own, one, one2, two, two2):
    return pl.pallas_call(
        near_kernel,
        in_specs=[SMEM, SMEM] + [HBM] * 6,
        out_specs=HBM,
        out_shape=jax.ShapeDtypeStruct((8, 2, 64, 256), F32),
        scratch_shapes=[
            pltpu.VMEM((8, 3, 2, 256, 512), BF16),
            pltpu.VMEM((24, 2, 64, 512), BF16),
            pltpu.VMEM((8, 2, 64, 256), F32),
            pltpu.SemaphoreType.DMA((8,)),
            pltpu.SemaphoreType.DMA((8,)),
            pltpu.SemaphoreType.DMA((5,)),
            pltpu.SemaphoreType.DMA((8,)),
        ],
        compiler_params=params(24),
        cost_estimate=cost(1 << 30, 1),
        name="near_field",
    )(links, places, in_hbm(near_blocks), in_hbm(own), one, one2, two, two2)


def gather_kernel(rel_ref, count_ref, ops_ref, after_ref, out_ref):
    del after_ref

    def box(b, carry):
        def entry(i, inner):
            out_ref[b, i] = ops_ref[rel_ref[b, i]].astype(F32)
            return inner

        lax.fori_loop(0, count_ref[b], entry, 0)
        return carry

    lax.fori_loop(0, 8, box, 0)


def gather_operators(rel, count, operators, after):
    return pl.pallas_call(
        gather_kernel,
        in_specs=[SMEM, SMEM, VMEM, ANYWHERE],
        out_specs=VMEM,
        out_shape=jax.ShapeDtypeStruct((8, 16, 2, 512), F32),
        compiler_params=params(8),
        cost_estimate=cost(1 << 20, 1),
        name="leaf_operators",
    )(rel, count, operators, after)


def links_kernel(src_ref, first_ref, after_ref, out_ref):
    del after_ref
    out_ref[...] = src_ref[...] - first_ref[0]


def link_offsets(src, first_box, after):
    return pl.pallas_call(
        links_kernel,
        in_specs=[VMEM, SMEM, ANYWHERE],
        out_specs=VMEM,
        out_shape=jax.ShapeDtypeStruct((8, 16), jnp.int32),
        compiler_params=params(4),
        cost_estimate=cost(1 << 34, 1),
        name="leaf_links",
    )(src, first_box, after)


def translate_kernel(
    first_row,
    place_ref,
    link_ref,
    count_ref,
    ops_ref,
    own_ref,
    one_ref,
    two_ref,
    *rest,
):
    out_hbm, boxes, wide, result, box_sems, out_sems = rest[-6:]
    one = pl.multiple_of(place_ref[1] * 16, 8)
    two = pl.multiple_of(16 - place_ref[1] * 16, 8)
    copies = [
        pltpu.make_async_copy(one_ref, boxes.at[pl.ds(one, 8)], box_sems.at[0]),
        pltpu.make_async_copy(own_ref, boxes.at[pl.ds(8, 8)], box_sems.at[1]),
        pltpu.make_async_copy(two_ref, boxes.at[pl.ds(two, 8)], box_sems.at[2]),
    ]
    for copy in copies:
        copy.start()

    def store(b):
        return pltpu.make_async_copy(
            result.at[b], out_hbm.at[b, :, pl.ds(first_row, 32), :], out_sems.at[b]
        )

    def box(b, carry):
        count = count_ref[b]

        def widen(i, inner):
            row = ops_ref[b, i]
            wide[i, 0] = jnp.broadcast_to(row[0:1], (16, 512)).astype(BF16)
            wide[i, 1] = jnp.broadcast_to(row[1:2], (16, 512)).astype(BF16)
            return inner

        lax.fori_loop(0, count, widen, 0)
        wide[count] = jnp.zeros((2, 16, 512), BF16)

        @pl.when(b == 0)
        def _():
            for copy in copies:
                copy.wait()

        def term(i):
            link = link_ref[b, jnp.minimum(i, 15)]
            real_part = boxes[link, 0].reshape(2, 16, 512)
            imag_part = boxes[link, 1].reshape(2, 16, 512)
            op_real = wide[i, 0][None]
            op_imag = wide[i, 1][None]
            return (
                op_real * real_part - op_imag * imag_part,
                op_real * imag_part + op_imag * real_part,
            )

        def pair(i, sums):
            real_one, imag_one = term(2 * i)
            real_two, imag_two = term(2 * i + 1)
            return (
                sums[0] + (real_one + real_two).reshape(32, 512).astype(F32),
                sums[1] + (imag_one + imag_two).reshape(32, 512).astype(F32),
            )

        zero = jnp.zeros((32, 512), F32)
        real_sum, imag_sum = lax.fori_loop(0, (count + 1) // 2, pair, (zero, zero))
        result[b, 0] = real_sum
        result[b, 1] = imag_sum
        store(b).start()
        return carry

    lax.fori_loop(0, 8, box, 0)
    for b in range(8):
        store(b).wait()


def leaf_translate(first_row, places, links, count, operators, own, one, two, partly=None):
    earlier = [] if partly is None else [partly]
    return pl.pallas_call(
        functools.partial(translate_kernel, first_row),
        in_specs=[SMEM] * 3 + [VMEM] + [ANYWHERE] * 3 + [HBM] * len(earlier),
        out_specs=HBM,
        out_shape=jax.ShapeDtypeStruct((8, 2, 64, 512), F32),
        scratch_shapes=[
            pltpu.VMEM((24, 2, 32, 512), BF16),
            pltpu.VMEM((18, 2, 16, 512), BF16),
            pltpu.VMEM((8, 2, 32, 512), F32),
            pltpu.SemaphoreType.DMA((3,)),
            pltpu.SemaphoreType.DMA((8,)),
        ],
        input_output_aliases={7: 0} if earlier else {},
        compiler_params=params(16),
        cost_estimate=cost(1 << 30, 1),
        name="leaf_translate",
    )(places, links, count, operators, own, one, two, *earlier)


def local(
    sources,
    near_blocks,
    near_src,
    radiation,
    il0_src,
    il0_rel,
    il0_count,
    trans0,
    phi_interp1,
    theta_interp1,
    shift1,
    phi_interp2,
    theta_interp2,
    shift2,
    il2_src,
    il2_rel,
    trans2,
):
    box_index = lax.axis_index(BOX)
    dir_position = lax.axis_index("dir")
    dir_index = dir_position.astype(jnp.int32).reshape(1)
    owners = lax.axis_size(BOX)
    first_box = (box_index - 1) * 8
    places = jnp.stack([dir_position, 1 - box_index % 2]).astype(jnp.int32)
    with_one = [(i, i ^ 1) for i in range(owners)]
    with_two = [(i, (i + 1 - 2 * ((i + 1) % 2)) % owners) for i in range(owners)]
    swap = [(0, 1), (1, 0)]

    half, send, low, high, mine = leaf_patterns(dir_index, sources, radiation)
    received = lax.ppermute(send, "dir", swap)
    two = lax.ppermute(half, BOX, with_two)
    one = lax.ppermute(half, BOX, with_one)
    two_swapped = lax.ppermute(two, "dir", swap)
    one_swapped = lax.ppermute(one, "dir", swap)
    mine, factors_two = lax.optimization_barrier((mine, shift2.reshape(8, 2, 64, 256)))
    level_one = level_one_patterns(dir_index, mine, received, phi_interp1, theta_interp1, shift1)

    kids = lax.all_to_all(level_one, ("xl", "z"), 0, 0, tiled=True)
    operators_two = upper_operators(il2_rel, trans2.reshape(316, 2, 128), level_one)
    low, near_links, operators_two = lax.optimization_barrier(
        (low, (near_src - first_box).astype(jnp.int32), operators_two)
    )
    low_two = lax.ppermute(low, BOX, with_two)
    low_one = lax.ppermute(low, BOX, with_one)
    near_field = near_products(near_links, places, near_blocks, sources, one, one_swapped, two, two_swapped)
    kids, near_field = lax.optimization_barrier((kids, near_field))
    terms = level_two_terms(kids, phi_interp2, theta_interp2, factors_two)

    got = lax.all_to_all(terms.reshape(128, 8, 128), ALL, 0, 0, tiled=True)
    links = link_offsets(il0_src, first_box.astype(jnp.int32).reshape(1), terms)
    high, links, rel = lax.optimization_barrier((high, links, il0_rel))
    high_two = lax.ppermute(high, BOX, with_two)
    high_one = lax.ppermute(high, BOX, with_one)
    operators = gather_operators(rel, il0_count, trans0, links)
    partly = leaf_translate(0, places, links, il0_count, operators, low, low_one, low_two)
    got, partly = lax.optimization_barrier((got, partly))
    upper = upper_translate(il2_src, got.reshape(8, 8, 2, 8, 128), operators_two)
    partly, upper = lax.optimization_barrier((partly, upper))
    leaf_incoming = leaf_translate(32, places, links, il0_count, operators, high, high_one, high_two, partly)
    return near_field, leaf_incoming, upper.reshape(8, 2, 64, 1, 128)


def solution(mesh):
    fine = Mesh(mesh.devices.reshape(4, 2, 2, 4, 2), ALL)
    placed = (
        P(BOX, None, None, None),
        P(BOX, None, None, "dir", None),
        P(BOX, None),
        P(BOX, None, None, "dir"),
        P(BOX, None),
        P(BOX, None),
        P(BOX),
        P(None, None, "dir"),
        P(),
        P(),
        P(),
        P(),
        P(),
        P(),
        P(),
        P(),
        P(None, None, BOX, "dir"),
    )
    return jax.shard_map(
        local,
        mesh=fine,
        in_specs=placed,
        out_specs=(
            P(BOX, None, None, "dir"),
            P(BOX, None, None, "dir"),
            P(None, None, None, BOX, "dir"),
        ),
        check_vma=False,
    )
```

```python
import jax
import jax.numpy as jnp
from jax import lax
from jax.experimental import pallas as pl
from jax.experimental.pallas import tpu as pltpu
from jax.sharding import Mesh
from jax.sharding import PartitionSpec as P

BOX = ("y", "xh", "xl", "z")
ALL = BOX + ("dir",)
F32 = jnp.float32
BF16 = jnp.bfloat16
HBM = pl.BlockSpec(memory_space=pltpu.HBM)
VMEM = pl.BlockSpec(memory_space=pltpu.VMEM)
SMEM = pl.BlockSpec(memory_space=pltpu.SMEM)
ANYWHERE = pl.BlockSpec(memory_space=pl.ANY)


def params(mebibytes):
    return pltpu.CompilerParams(vmem_limit_bytes=mebibytes << 20)


def cost(flops, nbytes):
    return pl.CostEstimate(flops=flops, bytes_accessed=nbytes, transcendentals=0)


def in_hbm(x):
    return pltpu.with_memory_space_constraint(x, pltpu.HBM)


def dot(a, b):
    return lax.dot_general(a, b, (((1,), (0,)), ((), ())), preferred_element_type=F32)


def dot_nt(a, b):
    return lax.dot_general(a, b, (((1,), (1,)), ((), ())), preferred_element_type=F32)


def leaf_kernel(
    dir_ref,
    src_hbm,
    rad_hbm,
    half_hbm,
    send_hbm,
    leaf,
    mine_ref,
    src,
    rad,
    src_sem,
    half_sem,
    rad_sems,
    send_sems,
):
    src_copy = pltpu.make_async_copy(src_hbm, src, src_sem)
    src_copy.start()
    for b in range(8):
        pltpu.make_async_copy(rad_hbm.at[b], rad.at[b], rad_sems.at[b]).start()
    src_copy.wait()
    first_box = pl.multiple_of(dir_ref[0] * 4, 4)
    half_copy = pltpu.make_async_copy(src.at[pl.ds(first_box, 4)], half_hbm, half_sem)
    half_copy.start()
    mine = pl.multiple_of(dir_ref[0] * 32, 32)
    other = pl.multiple_of((1 - dir_ref[0]) * 32, 32)

    def send(b):
        return pltpu.make_async_copy(leaf.at[b, :, pl.ds(other, 32), :], send_hbm.at[b], send_sems.at[b])

    def box(b, carry):
        pltpu.make_async_copy(rad_hbm.at[b], rad.at[b], rad_sems.at[b]).wait()
        rows = src[b].reshape(128, 512)
        first = dot(rows, rad[b, 0])
        second = dot(rows, rad[b, 1])
        leaf[b, 0] = (first[:64] - second[64:]).astype(BF16)
        leaf[b, 1] = (second[:64] + first[64:]).astype(BF16)
        send(b).start()
        mine_ref[b] = leaf[b, :, pl.ds(mine, 32), :]
        return carry

    lax.fori_loop(0, 8, box, 0)
    half_copy.wait()
    for b in range(8):
        send(b).wait()


def leaf_patterns(dir_index, sources, radiation):
    return pl.pallas_call(
        leaf_kernel,
        in_specs=[SMEM, HBM, HBM],
        out_specs=[HBM, HBM, VMEM, VMEM],
        out_shape=[
            pltpu.HBM((4, 2, 64, 512), BF16),
            pltpu.HBM((8, 2, 32, 512), BF16),
            jax.ShapeDtypeStruct((8, 2, 64, 512), BF16),
            jax.ShapeDtypeStruct((8, 2, 32, 512), BF16),
        ],
        scratch_shapes=[
            pltpu.VMEM((8, 2, 64, 512), BF16),
            pltpu.VMEM((8, 2, 512, 512), BF16),
            pltpu.SemaphoreType.DMA,
            pltpu.SemaphoreType.DMA,
            pltpu.SemaphoreType.DMA((8,)),
            pltpu.SemaphoreType.DMA((8,)),
        ],
        compiler_params=params(16),
        cost_estimate=cost(1, 1),
        name="leaf_patterns",
    )(dir_index, in_hbm(sources), in_hbm(radiation))


def level_one_kernel(
    dir_ref, mine_ref, other_ref, phi_ref, theta_ref, shift_ref, out_ref, expand, near, far, phi4, rows_f32
):
    step = pl.program_id(0)
    dir_index = dir_ref[0]

    @pl.when(step == 0)
    def _():
        spread = (
            lax.broadcasted_iota(jnp.int32, (32, 2048), 0)
            == lax.broadcasted_iota(jnp.int32, (32, 2048), 1) // 64
        ).astype(F32).astype(BF16)
        expand[...] = lax.dot_general(
            theta_ref[...], spread, (((0,), (0,)), ((), ())), preferred_element_type=F32
        )
        phi4[...] = jnp.zeros_like(phi4)
        for s in range(4):
            phi4[64 * s : 64 * s + 64, 128 * s : 128 * s + 128] = phi_ref[...]

    diagonal = (
        lax.broadcasted_iota(jnp.int32, (64, 256), 0) == lax.broadcasted_iota(jnp.int32, (64, 256), 1) % 64
    )
    near_rows = pl.multiple_of(dir_index * 8, 8)
    far_rows = pl.multiple_of((1 - dir_index) * 8, 8)
    for part in range(4):
        lanes = pl.ds(pl.multiple_of(step * 1024 + part * 256, 256), 256)
        near_values = expand[pl.ds(near_rows, 8), lanes]
        far_values = expand[pl.ds(far_rows, 8), lanes]
        for t in range(8):
            near[64 * t : 64 * t + 64, :] = jnp.where(diagonal, near_values[t : t + 1], 0.0).astype(BF16)
            far[64 * t : 64 * t + 64, :] = jnp.where(diagonal, far_values[t : t + 1], 0.0).astype(BF16)
        theta_out = dot(mine_ref[...].reshape(512, 512), near[...]) + dot(
            other_ref[...].reshape(512, 512), far[...]
        )
        fine = dot(theta_out.astype(BF16), phi4[...])
        real_sum = jnp.zeros((32, 512), F32)
        imag_sum = jnp.zeros((32, 512), F32)
        for b in range(8):
            real_part = fine[64 * b : 64 * b + 32]
            imag_part = fine[64 * b + 32 : 64 * b + 64]
            factors = shift_ref[b, :, 512 * part : 512 * part + 512].astype(F32)
            f_real, f_imag = factors[0:1], factors[1:2]
            real_sum = real_sum + (real_part * f_real - imag_part * f_imag)
            imag_sum = imag_sum + (real_part * f_imag + imag_part * f_real)
        for s in range(4):
            rows_f32[0:32, 4 * part + s, :] = real_sum[:, 128 * s : 128 * s + 128]
            rows_f32[32:64, 4 * part + s, :] = imag_sum[:, 128 * s : 128 * s + 128]
    for d in range(8):
        out_ref[d, 0] = rows_f32[4 * d : 4 * d + 4].astype(BF16)
        out_ref[d, 1] = rows_f32[32 + 4 * d : 36 + 4 * d].astype(BF16)


def level_one_patterns(dir_index, leaf, received, phi, theta, shift):
    return pl.pallas_call(
        level_one_kernel,
        grid_spec=pltpu.PrefetchScalarGridSpec(
            num_scalar_prefetch=1,
            grid=(2,),
            in_specs=[
                pl.BlockSpec((8, 2, 32, 512), lambda i, d: (0, 0, 0, 0)),
                pl.BlockSpec((8, 2, 32, 512), lambda i, d: (0, 0, 0, 0)),
                pl.BlockSpec((64, 128), lambda i, d: (0, 0)),
                pl.BlockSpec((32, 16), lambda i, d: (0, 0)),
                pl.BlockSpec((8, 2, 2048), lambda i, d: (0, 0, i)),
            ],
            out_specs=pl.BlockSpec((8, 2, 4, 16, 128), lambda i, d: (0, 0, 0, i, 0)),
            scratch_shapes=[
                pltpu.VMEM((16, 2048), F32),
                pltpu.VMEM((512, 256), BF16),
                pltpu.VMEM((512, 256), BF16),
                pltpu.VMEM((256, 512), BF16),
                pltpu.VMEM((64, 16, 128), F32),
            ],
        ),
        out_shape=jax.ShapeDtypeStruct((8, 2, 4, 32, 128), BF16),
        compiler_params=params(24),
        cost_estimate=cost(1, 1),
        name="level_one",
    )(dir_index, leaf, received, phi, theta, shift)


def level_two_kernel(kids_ref, phi_ref, theta_ref, shift_ref, out_ref, blocks, total, turned):
    tiled = dot(
        theta_ref[...],
        (
            lax.broadcasted_iota(jnp.int32, (32, 256), 0)
            == lax.broadcasted_iota(jnp.int32, (32, 256), 1) % 32
        ).astype(F32).astype(BF16),
    )
    owner = lax.broadcasted_iota(jnp.int32, (64, 256), 1) // 32
    for m in range(8):
        blocks[64 * m : 64 * m + 64, :] = jnp.where(owner == m, tiled, 0.0).astype(BF16)
    total[...] = jnp.zeros_like(total)

    def child(o, carry):
        along_phi = dot(kids_ref[o].reshape(256, 128), phi_ref[...]).astype(BF16)
        along_theta = dot(blocks[...], along_phi)
        f_real = shift_ref[o, 0].astype(F32)
        f_imag = shift_ref[o, 1].astype(F32)
        for r in range(4):
            real_part = along_theta[64 * r : 64 * r + 64]
            imag_part = along_theta[256 + 64 * r : 320 + 64 * r]
            total[r] = total[r] + (real_part * f_real - imag_part * f_imag)
            total[4 + r] = total[4 + r] + (real_part * f_imag + imag_part * f_real)
        return carry

    lax.fori_loop(0, 8, child, 0)
    for m in range(8):
        turned[:, m, :] = total[m]
    out_ref[:, 0] = turned[:, :, 0:128].astype(BF16)
    out_ref[:, 1] = turned[:, :, 128:256].astype(BF16)


def level_two_terms(kids, phi, theta, shift):
    return pl.pallas_call(
        level_two_kernel,
        out_shape=jax.ShapeDtypeStruct((64, 2, 8, 128), BF16),
        in_specs=[pl.BlockSpec(memory_space=pltpu.VMEM)] * 4,
        out_specs=pl.BlockSpec(memory_space=pltpu.VMEM),
        scratch_shapes=[
            pltpu.VMEM((512, 256), BF16),
            pltpu.VMEM((8, 64, 256), F32),
            pltpu.VMEM((64, 8, 256), F32),
        ],
        compiler_params=params(16),
        cost_estimate=cost(1, 1),
        name="level_two",
    )(kids, phi, theta, shift)


def upper_operators_kernel(rel_ref, ops_ref, after_ref, out_ref):
    del after_ref
    for h in range(8):
        for i in range(4):
            out_ref[h, i] = ops_ref[rel_ref[h, i]].astype(F32)


def upper_operators(rel, operators, after):
    return pl.pallas_call(
        upper_operators_kernel,
        in_specs=[SMEM, VMEM, ANYWHERE],
        out_specs=VMEM,
        out_shape=jax.ShapeDtypeStruct((8, 4, 2, 128), F32),
        compiler_params=params(8),
        cost_estimate=cost(1 << 34, 1),
        name="upper_operators",
    )(rel, operators, after)


def upper_kernel(src_ref, got_ref, ops_ref, out_ref, plain, rolled):
    for h in range(8):
        for g in range(8):
            for d in range(2):
                tile = got_ref[h, g, d].astype(F32)
                plain[h, 2 * g + d] = tile
                rolled[h, 2 * g + d] = pltpu.roll(tile, 4, 0)
    low = lax.broadcasted_iota(jnp.int32, (8, 128), 0) < 4

    def one(h, carry):
        total = jnp.zeros((16, 8, 128), F32)
        for i in range(4):
            operator = ops_ref[h, i]
            op_real = jnp.broadcast_to(operator[0:1], (8, 128))
            op_imag = jnp.broadcast_to(operator[1:2], (8, 128))
            op_imag = jnp.where(low, -op_imag, op_imag)
            src = src_ref[h, i]
            total = total + (plain[src] * op_real[None] + rolled[src] * op_imag[None])
        for g in range(8):
            for d in range(2):
                start = 32 * d + 4 * g
                out_ref[h, 0, start : start + 4, :] = total[2 * g + d, 0:4]
                out_ref[h, 1, start : start + 4, :] = total[2 * g + d, 4:8]
        return carry

    lax.fori_loop(0, 8, one, 0)


def upper_translate(il2_src, got, operators):
    return pl.pallas_call(
        upper_kernel,
        out_shape=jax.ShapeDtypeStruct((8, 2, 64, 128), F32),
        in_specs=[SMEM, VMEM, VMEM],
        out_specs=VMEM,
        scratch_shapes=[pltpu.VMEM((8, 16, 8, 128), F32), pltpu.VMEM((8, 16, 8, 128), F32)],
        compiler_params=params(12),
        cost_estimate=cost(1 << 34, 1),
        name="upper_translate",
    )(il2_src, got, operators)


def near_kernel(
    link_ref,
    place_ref,
    blocks_hbm,
    own_hbm,
    one_hbm,
    one2_hbm,
    two_hbm,
    two2_hbm,
    out_hbm,
    blocks,
    boxes,
    result,
    self_sems,
    block_sems,
    box_sems,
    out_sems,
):
    mine = place_ref[0] * 4
    theirs = 4 - mine
    one = place_ref[1] * 16
    two = 16 - one

    def beside(source, start, sem):
        return pltpu.make_async_copy(source, boxes.at[pl.ds(pl.multiple_of(start, 4), 4)], box_sems.at[sem])

    def self_block(b):
        return pltpu.make_async_copy(blocks_hbm.at[b, 0], blocks.at[b, 0], self_sems.at[b])

    def other_blocks(b):
        rest = pl.ds(1, 2)
        return pltpu.make_async_copy(blocks_hbm.at[b, rest], blocks.at[b, rest], block_sems.at[b])

    own_copy = pltpu.make_async_copy(own_hbm, boxes.at[pl.ds(8, 8)], box_sems.at[4])
    own_copy.start()
    for b in range(8):
        self_block(b).start()
    copies = [
        beside(one_hbm, one + mine, 0),
        beside(one2_hbm, one + theirs, 1),
        beside(two_hbm, two + mine, 2),
        beside(two2_hbm, two + theirs, 3),
    ]
    for copy in copies:
        copy.start()
    for b in range(8):
        other_blocks(b).start()

    def product(b, j, box):
        rows = boxes[box].reshape(128, 512)
        first = dot_nt(rows, blocks[b, j, 0])
        second = dot_nt(rows, blocks[b, j, 1])
        return first[:64] - second[64:], second[:64] + first[64:]

    own_copy.wait()

    def itself(b, carry):
        self_block(b).wait()
        result[b, 0], result[b, 1] = product(b, 0, link_ref[b, 0])
        return carry

    lax.fori_loop(0, 8, itself, 0)
    for copy in copies:
        copy.wait()

    def others(b, carry):
        other_blocks(b).wait()
        real_one, imag_one = product(b, 1, link_ref[b, 1])
        real_two, imag_two = product(b, 2, link_ref[b, 2])
        result[b, 0] = result[b, 0] + (real_one + real_two)
        result[b, 1] = result[b, 1] + (imag_one + imag_two)
        pltpu.make_async_copy(result.at[b], out_hbm.at[b], out_sems.at[b]).start()
        return carry

    lax.fori_loop(0, 8, others, 0)
    for b in range(8):
        pltpu.make_async_copy(result.at[b], out_hbm.at[b], out_sems.at[b]).wait()


def near_products(links, places, near_blocks, own, one, one2, two, two2):
    return pl.pallas_call(
        near_kernel,
        in_specs=[SMEM, SMEM] + [HBM] * 6,
        out_specs=HBM,
        out_shape=jax.ShapeDtypeStruct((8, 2, 64, 256), F32),
        scratch_shapes=[
            pltpu.VMEM((8, 3, 2, 256, 512), BF16),
            pltpu.VMEM((24, 2, 64, 512), BF16),
            pltpu.VMEM((8, 2, 64, 256), F32),
            pltpu.SemaphoreType.DMA((8,)),
            pltpu.SemaphoreType.DMA((8,)),
            pltpu.SemaphoreType.DMA((5,)),
            pltpu.SemaphoreType.DMA((8,)),
        ],
        compiler_params=params(24),
        cost_estimate=cost(1 << 30, 1),
        name="near_field",
    )(links, places, in_hbm(near_blocks), in_hbm(own), one, one2, two, two2)


def gather_kernel(rel_ref, count_ref, ops_ref, after_ref, out_ref):
    del after_ref

    def box(b, carry):
        def entry(i, inner):
            out_ref[b, i] = ops_ref[rel_ref[b, i]].astype(F32)
            return inner

        lax.fori_loop(0, count_ref[b], entry, 0)
        return carry

    lax.fori_loop(0, 8, box, 0)


def gather_operators(rel, count, operators, after):
    return pl.pallas_call(
        gather_kernel,
        in_specs=[SMEM, SMEM, VMEM, ANYWHERE],
        out_specs=VMEM,
        out_shape=jax.ShapeDtypeStruct((8, 16, 2, 512), F32),
        compiler_params=params(8),
        cost_estimate=cost(1 << 20, 1),
        name="leaf_operators",
    )(rel, count, operators, after)


def links_kernel(src_ref, first_ref, after_ref, out_ref):
    del after_ref
    out_ref[...] = src_ref[...] - first_ref[0]


def link_offsets(src, first_box, after):
    return pl.pallas_call(
        links_kernel,
        in_specs=[VMEM, SMEM, ANYWHERE],
        out_specs=VMEM,
        out_shape=jax.ShapeDtypeStruct((8, 16), jnp.int32),
        compiler_params=params(4),
        cost_estimate=cost(1 << 34, 1),
        name="leaf_links",
    )(src, first_box, after)


def translate_kernel(
    place_ref,
    link_ref,
    count_ref,
    ops_ref,
    own_ref,
    one_ref,
    two_ref,
    out_hbm,
    boxes,
    wide,
    result,
    box_sems,
    out_sems,
):
    one = pl.multiple_of(place_ref[1] * 16, 8)
    two = pl.multiple_of(16 - place_ref[1] * 16, 8)
    copies = [
        pltpu.make_async_copy(one_ref, boxes.at[pl.ds(one, 8)], box_sems.at[0]),
        pltpu.make_async_copy(own_ref, boxes.at[pl.ds(8, 8)], box_sems.at[1]),
        pltpu.make_async_copy(two_ref, boxes.at[pl.ds(two, 8)], box_sems.at[2]),
    ]
    for copy in copies:
        copy.start()

    def store(b):
        return pltpu.make_async_copy(result.at[b], out_hbm.at[b], out_sems.at[b])

    def box(b, carry):
        count = count_ref[b]

        def widen(i, inner):
            row = ops_ref[b, i]
            wide[i, 0] = jnp.broadcast_to(row[0:1], (16, 512)).astype(BF16)
            wide[i, 1] = jnp.broadcast_to(row[1:2], (16, 512)).astype(BF16)
            return inner

        lax.fori_loop(0, count, widen, 0)
        wide[count] = jnp.zeros((2, 16, 512), BF16)

        @pl.when(b == 0)
        def _():
            for copy in copies:
                copy.wait()

        for start in range(0, 64, 32):
            size = 32
            chunk = slice(start, start + size)

            def term(i):
                link = link_ref[b, jnp.minimum(i, 15)]
                real_part = boxes[link, 0, chunk, :].reshape(size // 16, 16, 512)
                imag_part = boxes[link, 1, chunk, :].reshape(size // 16, 16, 512)
                op_real = wide[i, 0][None]
                op_imag = wide[i, 1][None]
                return (
                    op_real * real_part - op_imag * imag_part,
                    op_real * imag_part + op_imag * real_part,
                )

            def pair(i, sums):
                real_one, imag_one = term(2 * i)
                real_two, imag_two = term(2 * i + 1)
                return (
                    sums[0] + (real_one + real_two).reshape(size, 512).astype(F32),
                    sums[1] + (imag_one + imag_two).reshape(size, 512).astype(F32),
                )

            zero = jnp.zeros((size, 512), F32)
            real_sum, imag_sum = lax.fori_loop(0, (count + 1) // 2, pair, (zero, zero))
            result[b, 0, chunk, :] = real_sum
            result[b, 1, chunk, :] = imag_sum
        store(b).start()
        return carry

    lax.fori_loop(0, 8, box, 0)
    for b in range(8):
        store(b).wait()


def leaf_translate(places, links, count, operators, own, one, two):
    return pl.pallas_call(
        translate_kernel,
        in_specs=[SMEM] * 3 + [VMEM] + [ANYWHERE] * 3,
        out_specs=HBM,
        out_shape=jax.ShapeDtypeStruct((8, 2, 64, 512), F32),
        scratch_shapes=[
            pltpu.VMEM((24, 2, 64, 512), BF16),
            pltpu.VMEM((18, 2, 16, 512), BF16),
            pltpu.VMEM((8, 2, 64, 512), F32),
            pltpu.SemaphoreType.DMA((3,)),
            pltpu.SemaphoreType.DMA((8,)),
        ],
        compiler_params=params(16),
        cost_estimate=cost(1 << 30, 1),
        name="leaf_translate",
    )(places, links, count, operators, own, one, two)


def local(
    sources,
    near_blocks,
    near_src,
    radiation,
    il0_src,
    il0_rel,
    il0_count,
    trans0,
    phi_interp1,
    theta_interp1,
    shift1,
    phi_interp2,
    theta_interp2,
    shift2,
    il2_src,
    il2_rel,
    trans2,
):
    box_index = lax.axis_index(BOX)
    dir_position = lax.axis_index("dir")
    dir_index = dir_position.astype(jnp.int32).reshape(1)
    owners = lax.axis_size(BOX)
    first_box = (box_index - 1) * 8
    places = jnp.stack([dir_position, 1 - box_index % 2]).astype(jnp.int32)
    with_one = [(i, i ^ 1) for i in range(owners)]
    with_two = [(i, i + 1 - 2 * ((i + 1) % 2)) for i in range(1, owners - 1)]
    swap = [(0, 1), (1, 0)]

    half, send, leaf, mine = leaf_patterns(dir_index, sources, radiation)
    received = lax.ppermute(send, "dir", swap)
    two = lax.ppermute(half, BOX, with_two)
    one = lax.ppermute(half, BOX, with_one)
    two_swapped = lax.ppermute(two, "dir", swap)
    one_swapped = lax.ppermute(one, "dir", swap)
    mine, factors_two = lax.optimization_barrier((mine, shift2.reshape(8, 2, 64, 256)))
    level_one = level_one_patterns(dir_index, mine, received, phi_interp1, theta_interp1, shift1)

    kids = lax.all_to_all(level_one, ("xl", "z"), 0, 0, tiled=True)
    operators_two = upper_operators(il2_rel, trans2.reshape(316, 2, 128), level_one)
    leaf, near_links, operators_two = lax.optimization_barrier(
        (leaf, (near_src - first_box).astype(jnp.int32), operators_two)
    )
    leaf_two = lax.ppermute(leaf, BOX, with_two)
    leaf_one = lax.ppermute(leaf, BOX, with_one)
    near_field = near_products(near_links, places, near_blocks, sources, one, one_swapped, two, two_swapped)
    kids, near_field = lax.optimization_barrier((kids, near_field))
    terms = level_two_terms(kids, phi_interp2, theta_interp2, factors_two)

    got = lax.all_to_all(terms.reshape(128, 8, 128), ALL, 0, 0, tiled=True)
    links = link_offsets(il0_src, first_box.astype(jnp.int32).reshape(1), terms)
    operators = gather_operators(il0_rel, il0_count, trans0, links)
    leaf_incoming = leaf_translate(places, links, il0_count, operators, leaf, leaf_one, leaf_two)
    got, leaf_incoming = lax.optimization_barrier((got, leaf_incoming))
    upper = upper_translate(il2_src, got.reshape(8, 8, 2, 8, 128), operators_two)
    return near_field, leaf_incoming, upper.reshape(8, 2, 64, 1, 128)


def solution(mesh):
    fine = Mesh(mesh.devices.reshape(4, 2, 2, 4, 2), ALL)
    placed = (
        P(BOX, None, None, None),
        P(BOX, None, None, "dir", None),
        P(BOX, None),
        P(BOX, None, None, "dir"),
        P(BOX, None),
        P(BOX, None),
        P(BOX),
        P(None, None, "dir"),
        P(),
        P(),
        P(),
        P(),
        P(),
        P(),
        P(),
        P(),
        P(None, None, BOX, "dir"),
    )
    return jax.shard_map(
        local,
        mesh=fine,
        in_specs=placed,
        out_specs=(
            P(BOX, None, None, "dir"),
            P(BOX, None, None, "dir"),
            P(None, None, None, BOX, "dir"),
        ),
        check_vma=False,
    )
```

```python
import jax
import jax.numpy as jnp
from jax import lax
from jax.experimental import pallas as pl
from jax.experimental.pallas import tpu as pltpu
from jax.sharding import Mesh
from jax.sharding import PartitionSpec as P

BOX = ("y", "xh", "xl", "z")
ALL = BOX + ("dir",)
F32 = jnp.float32
BF16 = jnp.bfloat16
HBM = pl.BlockSpec(memory_space=pltpu.HBM)
VMEM = pl.BlockSpec(memory_space=pltpu.VMEM)
SMEM = pl.BlockSpec(memory_space=pltpu.SMEM)
ANYWHERE = pl.BlockSpec(memory_space=pl.ANY)


def params(mebibytes):
    return pltpu.CompilerParams(vmem_limit_bytes=mebibytes << 20)


def cost(flops, nbytes):
    return pl.CostEstimate(flops=flops, bytes_accessed=nbytes, transcendentals=0)


def in_hbm(x):
    return pltpu.with_memory_space_constraint(x, pltpu.HBM)


def dot(a, b):
    return lax.dot_general(a, b, (((1,), (0,)), ((), ())), preferred_element_type=F32)


def dot_nt(a, b):
    return lax.dot_general(a, b, (((1,), (1,)), ((), ())), preferred_element_type=F32)


def leaf_kernel(
    dir_ref,
    src_hbm,
    rad_hbm,
    half_hbm,
    send_hbm,
    leaf,
    mine_ref,
    src,
    rad,
    src_sem,
    half_sem,
    rad_sems,
    send_sems,
):
    src_copy = pltpu.make_async_copy(src_hbm, src, src_sem)
    src_copy.start()
    for b in range(8):
        pltpu.make_async_copy(rad_hbm.at[b], rad.at[b], rad_sems.at[b]).start()
    src_copy.wait()
    first_box = pl.multiple_of(dir_ref[0] * 4, 4)
    half_copy = pltpu.make_async_copy(src.at[pl.ds(first_box, 4)], half_hbm, half_sem)
    half_copy.start()
    mine = pl.multiple_of(dir_ref[0] * 32, 32)
    other = pl.multiple_of((1 - dir_ref[0]) * 32, 32)

    def send(b):
        return pltpu.make_async_copy(leaf.at[b, :, pl.ds(other, 32), :], send_hbm.at[b], send_sems.at[b])

    def box(b, carry):
        pltpu.make_async_copy(rad_hbm.at[b], rad.at[b], rad_sems.at[b]).wait()
        rows = src[b].reshape(128, 512)
        first = dot(rows, rad[b, 0])
        second = dot(rows, rad[b, 1])
        leaf[b, 0] = (first[:64] - second[64:]).astype(BF16)
        leaf[b, 1] = (second[:64] + first[64:]).astype(BF16)
        send(b).start()
        mine_ref[b] = leaf[b, :, pl.ds(mine, 32), :]
        return carry

    lax.fori_loop(0, 8, box, 0)
    half_copy.wait()
    for b in range(8):
        send(b).wait()


def leaf_patterns(dir_index, sources, radiation):
    return pl.pallas_call(
        leaf_kernel,
        in_specs=[SMEM, HBM, HBM],
        out_specs=[HBM, HBM, VMEM, VMEM],
        out_shape=[
            pltpu.HBM((4, 2, 64, 512), BF16),
            pltpu.HBM((8, 2, 32, 512), BF16),
            jax.ShapeDtypeStruct((8, 2, 64, 512), BF16),
            jax.ShapeDtypeStruct((8, 2, 32, 512), BF16),
        ],
        scratch_shapes=[
            pltpu.VMEM((8, 2, 64, 512), BF16),
            pltpu.VMEM((8, 2, 512, 512), BF16),
            pltpu.SemaphoreType.DMA,
            pltpu.SemaphoreType.DMA,
            pltpu.SemaphoreType.DMA((8,)),
            pltpu.SemaphoreType.DMA((8,)),
        ],
        compiler_params=params(16),
        cost_estimate=cost(1, 1),
        name="leaf_patterns",
    )(dir_index, in_hbm(sources), in_hbm(radiation))


def level_one_kernel(
    dir_ref, mine_ref, other_ref, phi_ref, theta_ref, shift_ref, out_ref, expand, near, far, phi4, rows_f32
):
    step = pl.program_id(0)
    dir_index = dir_ref[0]

    @pl.when(step == 0)
    def _():
        spread = (
            lax.broadcasted_iota(jnp.int32, (32, 2048), 0)
            == lax.broadcasted_iota(jnp.int32, (32, 2048), 1) // 64
        ).astype(F32).astype(BF16)
        expand[...] = lax.dot_general(
            theta_ref[...], spread, (((0,), (0,)), ((), ())), preferred_element_type=F32
        )
        phi4[...] = jnp.zeros_like(phi4)
        for s in range(4):
            phi4[64 * s : 64 * s + 64, 128 * s : 128 * s + 128] = phi_ref[...]

    diagonal = (
        lax.broadcasted_iota(jnp.int32, (64, 256), 0) == lax.broadcasted_iota(jnp.int32, (64, 256), 1) % 64
    )
    near_rows = pl.multiple_of(dir_index * 8, 8)
    far_rows = pl.multiple_of((1 - dir_index) * 8, 8)
    for part in range(4):
        lanes = pl.ds(pl.multiple_of(step * 1024 + part * 256, 256), 256)
        near_values = expand[pl.ds(near_rows, 8), lanes]
        far_values = expand[pl.ds(far_rows, 8), lanes]
        for t in range(8):
            near[64 * t : 64 * t + 64, :] = jnp.where(diagonal, near_values[t : t + 1], 0.0).astype(BF16)
            far[64 * t : 64 * t + 64, :] = jnp.where(diagonal, far_values[t : t + 1], 0.0).astype(BF16)
        theta_out = dot(mine_ref[...].reshape(512, 512), near[...]) + dot(
            other_ref[...].reshape(512, 512), far[...]
        )
        fine = dot(theta_out.astype(BF16), phi4[...])
        real_sum = jnp.zeros((32, 512), F32)
        imag_sum = jnp.zeros((32, 512), F32)
        for b in range(8):
            real_part = fine[64 * b : 64 * b + 32]
            imag_part = fine[64 * b + 32 : 64 * b + 64]
            factors = shift_ref[b, :, 512 * part : 512 * part + 512].astype(F32)
            f_real, f_imag = factors[0:1], factors[1:2]
            real_sum = real_sum + (real_part * f_real - imag_part * f_imag)
            imag_sum = imag_sum + (real_part * f_imag + imag_part * f_real)
        for s in range(4):
            rows_f32[0:32, 4 * part + s, :] = real_sum[:, 128 * s : 128 * s + 128]
            rows_f32[32:64, 4 * part + s, :] = imag_sum[:, 128 * s : 128 * s + 128]
    for d in range(8):
        out_ref[d, 0] = rows_f32[4 * d : 4 * d + 4].astype(BF16)
        out_ref[d, 1] = rows_f32[32 + 4 * d : 36 + 4 * d].astype(BF16)


def level_one_patterns(dir_index, leaf, received, phi, theta, shift):
    return pl.pallas_call(
        level_one_kernel,
        grid_spec=pltpu.PrefetchScalarGridSpec(
            num_scalar_prefetch=1,
            grid=(2,),
            in_specs=[
                pl.BlockSpec((8, 2, 32, 512), lambda i, d: (0, 0, 0, 0)),
                pl.BlockSpec((8, 2, 32, 512), lambda i, d: (0, 0, 0, 0)),
                pl.BlockSpec((64, 128), lambda i, d: (0, 0)),
                pl.BlockSpec((32, 16), lambda i, d: (0, 0)),
                pl.BlockSpec((8, 2, 2048), lambda i, d: (0, 0, i)),
            ],
            out_specs=pl.BlockSpec((8, 2, 4, 16, 128), lambda i, d: (0, 0, 0, i, 0)),
            scratch_shapes=[
                pltpu.VMEM((16, 2048), F32),
                pltpu.VMEM((512, 256), BF16),
                pltpu.VMEM((512, 256), BF16),
                pltpu.VMEM((256, 512), BF16),
                pltpu.VMEM((64, 16, 128), F32),
            ],
        ),
        out_shape=jax.ShapeDtypeStruct((8, 2, 4, 32, 128), BF16),
        compiler_params=params(24),
        cost_estimate=cost(1, 1),
        name="level_one",
    )(dir_index, leaf, received, phi, theta, shift)


def level_two_kernel(kids_ref, phi_ref, theta_ref, shift_ref, out_ref, blocks, total, turned):
    tiled = dot(
        theta_ref[...],
        (
            lax.broadcasted_iota(jnp.int32, (32, 256), 0)
            == lax.broadcasted_iota(jnp.int32, (32, 256), 1) % 32
        ).astype(F32).astype(BF16),
    )
    owner = lax.broadcasted_iota(jnp.int32, (64, 256), 1) // 32
    for m in range(8):
        blocks[64 * m : 64 * m + 64, :] = jnp.where(owner == m, tiled, 0.0).astype(BF16)
    total[...] = jnp.zeros_like(total)

    def child(o, carry):
        along_phi = dot(kids_ref[o].reshape(256, 128), phi_ref[...]).astype(BF16)
        along_theta = dot(blocks[...], along_phi)
        f_real = shift_ref[o, 0].astype(F32)
        f_imag = shift_ref[o, 1].astype(F32)
        for r in range(4):
            real_part = along_theta[64 * r : 64 * r + 64]
            imag_part = along_theta[256 + 64 * r : 320 + 64 * r]
            total[r] = total[r] + (real_part * f_real - imag_part * f_imag)
            total[4 + r] = total[4 + r] + (real_part * f_imag + imag_part * f_real)
        return carry

    lax.fori_loop(0, 8, child, 0)
    for m in range(8):
        turned[:, m, :] = total[m]
    out_ref[:, 0] = turned[:, :, 0:128].astype(BF16)
    out_ref[:, 1] = turned[:, :, 128:256].astype(BF16)


def level_two_terms(kids, phi, theta, shift):
    return pl.pallas_call(
        level_two_kernel,
        out_shape=jax.ShapeDtypeStruct((64, 2, 8, 128), BF16),
        in_specs=[pl.BlockSpec(memory_space=pltpu.VMEM)] * 4,
        out_specs=pl.BlockSpec(memory_space=pltpu.VMEM),
        scratch_shapes=[
            pltpu.VMEM((512, 256), BF16),
            pltpu.VMEM((8, 64, 256), F32),
            pltpu.VMEM((64, 8, 256), F32),
        ],
        compiler_params=params(16),
        cost_estimate=cost(1, 1),
        name="level_two",
    )(kids, phi, theta, shift)


def upper_operators_kernel(rel_ref, ops_ref, after_ref, out_ref):
    del after_ref
    for h in range(8):
        for i in range(4):
            out_ref[h, i] = ops_ref[rel_ref[h, i]].astype(F32)


def upper_operators(rel, operators, after):
    return pl.pallas_call(
        upper_operators_kernel,
        in_specs=[SMEM, VMEM, ANYWHERE],
        out_specs=VMEM,
        out_shape=jax.ShapeDtypeStruct((8, 4, 2, 128), F32),
        compiler_params=params(8),
        cost_estimate=cost(1 << 34, 1),
        name="upper_operators",
    )(rel, operators, after)


def upper_kernel(src_ref, got_ref, ops_ref, out_ref, plain, rolled):
    for h in range(8):
        for g in range(8):
            for d in range(2):
                tile = got_ref[h, g, d].astype(F32)
                plain[h, 2 * g + d] = tile
                rolled[h, 2 * g + d] = pltpu.roll(tile, 4, 0)
    low = lax.broadcasted_iota(jnp.int32, (8, 128), 0) < 4

    def one(h, carry):
        total = jnp.zeros((16, 8, 128), F32)
        for i in range(4):
            operator = ops_ref[h, i]
            op_real = jnp.broadcast_to(operator[0:1], (8, 128))
            op_imag = jnp.broadcast_to(operator[1:2], (8, 128))
            op_imag = jnp.where(low, -op_imag, op_imag)
            src = src_ref[h, i]
            total = total + (plain[src] * op_real[None] + rolled[src] * op_imag[None])
        for g in range(8):
            for d in range(2):
                start = 32 * d + 4 * g
                out_ref[h, 0, start : start + 4, :] = total[2 * g + d, 0:4]
                out_ref[h, 1, start : start + 4, :] = total[2 * g + d, 4:8]
        return carry

    lax.fori_loop(0, 8, one, 0)


def upper_translate(il2_src, got, operators):
    return pl.pallas_call(
        upper_kernel,
        out_shape=jax.ShapeDtypeStruct((8, 2, 64, 128), F32),
        in_specs=[SMEM, VMEM, VMEM],
        out_specs=VMEM,
        scratch_shapes=[pltpu.VMEM((8, 16, 8, 128), F32), pltpu.VMEM((8, 16, 8, 128), F32)],
        compiler_params=params(12),
        cost_estimate=cost(1 << 34, 1),
        name="upper_translate",
    )(il2_src, got, operators)


def near_kernel(
    link_ref,
    place_ref,
    blocks_hbm,
    own_hbm,
    one_hbm,
    one2_hbm,
    two_hbm,
    two2_hbm,
    out_hbm,
    blocks,
    boxes,
    result,
    self_sems,
    block_sems,
    box_sems,
    out_sems,
):
    mine = place_ref[0] * 4
    theirs = 4 - mine
    one = place_ref[1] * 16
    two = 16 - one

    def beside(source, start, sem):
        return pltpu.make_async_copy(source, boxes.at[pl.ds(pl.multiple_of(start, 4), 4)], box_sems.at[sem])

    def self_block(b):
        return pltpu.make_async_copy(blocks_hbm.at[b, 0], blocks.at[b, 0], self_sems.at[b])

    def other_blocks(b):
        rest = pl.ds(1, 2)
        return pltpu.make_async_copy(blocks_hbm.at[b, rest], blocks.at[b, rest], block_sems.at[b])

    own_copy = pltpu.make_async_copy(own_hbm, boxes.at[pl.ds(8, 8)], box_sems.at[4])
    own_copy.start()
    for b in range(8):
        self_block(b).start()
    copies = [
        beside(one_hbm, one + mine, 0),
        beside(one2_hbm, one + theirs, 1),
        beside(two_hbm, two + mine, 2),
        beside(two2_hbm, two + theirs, 3),
    ]
    for copy in copies:
        copy.start()
    for b in range(8):
        other_blocks(b).start()

    def product(b, j, box):
        rows = boxes[box].reshape(128, 512)
        first = dot_nt(rows, blocks[b, j, 0])
        second = dot_nt(rows, blocks[b, j, 1])
        return first[:64] - second[64:], second[:64] + first[64:]

    own_copy.wait()

    def itself(b, carry):
        self_block(b).wait()
        result[b, 0], result[b, 1] = product(b, 0, link_ref[b, 0])
        return carry

    lax.fori_loop(0, 8, itself, 0)
    for copy in copies:
        copy.wait()

    def others(b, carry):
        other_blocks(b).wait()
        real_one, imag_one = product(b, 1, link_ref[b, 1])
        real_two, imag_two = product(b, 2, link_ref[b, 2])
        result[b, 0] = result[b, 0] + (real_one + real_two)
        result[b, 1] = result[b, 1] + (imag_one + imag_two)
        pltpu.make_async_copy(result.at[b], out_hbm.at[b], out_sems.at[b]).start()
        return carry

    lax.fori_loop(0, 8, others, 0)
    for b in range(8):
        pltpu.make_async_copy(result.at[b], out_hbm.at[b], out_sems.at[b]).wait()


def near_products(links, places, near_blocks, own, one, one2, two, two2):
    return pl.pallas_call(
        near_kernel,
        in_specs=[SMEM, SMEM] + [HBM] * 6,
        out_specs=HBM,
        out_shape=jax.ShapeDtypeStruct((8, 2, 64, 256), F32),
        scratch_shapes=[
            pltpu.VMEM((8, 3, 2, 256, 512), BF16),
            pltpu.VMEM((24, 2, 64, 512), BF16),
            pltpu.VMEM((8, 2, 64, 256), F32),
            pltpu.SemaphoreType.DMA((8,)),
            pltpu.SemaphoreType.DMA((8,)),
            pltpu.SemaphoreType.DMA((5,)),
            pltpu.SemaphoreType.DMA((8,)),
        ],
        compiler_params=params(24),
        cost_estimate=cost(1 << 30, 1),
        name="near_field",
    )(links, places, near_blocks, in_hbm(own), one, one2, two, two2)


def gather_kernel(rel_ref, count_ref, ops_ref, after_ref, out_ref):
    del after_ref

    def box(b, carry):
        def entry(i, inner):
            row = ops_ref[rel_ref[b, i]].astype(F32)
            out_ref[b, i, 0] = jnp.broadcast_to(row[0:1], (16, 512)).astype(BF16)
            out_ref[b, i, 1] = jnp.broadcast_to(row[1:2], (16, 512)).astype(BF16)
            return inner

        count = count_ref[b]
        lax.fori_loop(0, count, entry, 0)
        out_ref[b, count] = jnp.zeros((2, 16, 512), BF16)
        return carry

    lax.fori_loop(0, 8, box, 0)


def gather_operators(rel, count, operators, after):
    return pl.pallas_call(
        gather_kernel,
        in_specs=[SMEM, SMEM, VMEM, ANYWHERE],
        out_specs=VMEM,
        out_shape=jax.ShapeDtypeStruct((8, 17, 2, 16, 512), BF16),
        compiler_params=params(12),
        cost_estimate=cost(1 << 20, 1),
        name="leaf_operators",
    )(rel, count, operators, after)


def links_kernel(src_ref, first_ref, after_ref, out_ref):
    del after_ref
    out_ref[...] = src_ref[...] - first_ref[0]


def link_offsets(src, first_box, after):
    return pl.pallas_call(
        links_kernel,
        in_specs=[VMEM, SMEM, ANYWHERE],
        out_specs=VMEM,
        out_shape=jax.ShapeDtypeStruct((8, 16), jnp.int32),
        compiler_params=params(4),
        cost_estimate=cost(1 << 34, 1),
        name="leaf_links",
    )(src, first_box, after)


def translate_kernel(
    place_ref,
    link_ref,
    count_ref,
    ops_ref,
    own_ref,
    one_ref,
    two_ref,
    out_hbm,
    boxes,
    result,
    box_sems,
    out_sems,
):
    one = pl.multiple_of(place_ref[1] * 16, 8)
    two = pl.multiple_of(16 - place_ref[1] * 16, 8)
    copies = [
        pltpu.make_async_copy(one_ref, boxes.at[pl.ds(one, 8)], box_sems.at[0]),
        pltpu.make_async_copy(own_ref, boxes.at[pl.ds(8, 8)], box_sems.at[1]),
        pltpu.make_async_copy(two_ref, boxes.at[pl.ds(two, 8)], box_sems.at[2]),
    ]
    for copy in copies:
        copy.start()

    def store(b):
        return pltpu.make_async_copy(result.at[b], out_hbm.at[b], out_sems.at[b])

    def box(b, carry):
        count = count_ref[b]

        @pl.when(b == 0)
        def _():
            for copy in copies:
                copy.wait()

        for start in range(0, 64, 32):
            size = 32
            chunk = slice(start, start + size)

            def term(i):
                link = link_ref[b, jnp.minimum(i, 15)]
                real_part = boxes[link, 0, chunk, :].reshape(size // 16, 16, 512)
                imag_part = boxes[link, 1, chunk, :].reshape(size // 16, 16, 512)
                op_real = ops_ref[b, i, 0][None]
                op_imag = ops_ref[b, i, 1][None]
                return (
                    op_real * real_part - op_imag * imag_part,
                    op_real * imag_part + op_imag * real_part,
                )

            def pair(i, sums):
                real_one, imag_one = term(2 * i)
                real_two, imag_two = term(2 * i + 1)
                return (
                    sums[0] + (real_one + real_two).reshape(size, 512).astype(F32),
                    sums[1] + (imag_one + imag_two).reshape(size, 512).astype(F32),
                )

            zero = jnp.zeros((size, 512), F32)
            real_sum, imag_sum = lax.fori_loop(0, (count + 1) // 2, pair, (zero, zero))
            result[b, 0, chunk, :] = real_sum
            result[b, 1, chunk, :] = imag_sum
        store(b).start()
        return carry

    lax.fori_loop(0, 8, box, 0)
    for b in range(8):
        store(b).wait()


def leaf_translate(places, links, count, operators, own, one, two):
    return pl.pallas_call(
        translate_kernel,
        in_specs=[SMEM] * 3 + [VMEM] + [ANYWHERE] * 3,
        out_specs=HBM,
        out_shape=jax.ShapeDtypeStruct((8, 2, 64, 512), F32),
        scratch_shapes=[
            pltpu.VMEM((24, 2, 64, 512), BF16),
            pltpu.VMEM((8, 2, 64, 512), F32),
            pltpu.SemaphoreType.DMA((3,)),
            pltpu.SemaphoreType.DMA((8,)),
        ],
        compiler_params=params(16),
        cost_estimate=cost(1 << 30, 1),
        name="leaf_translate",
    )(places, links, count, operators, own, one, two)


def local(
    sources,
    near_blocks,
    near_src,
    radiation,
    il0_src,
    il0_rel,
    il0_count,
    trans0,
    phi_interp1,
    theta_interp1,
    shift1,
    phi_interp2,
    theta_interp2,
    shift2,
    il2_src,
    il2_rel,
    trans2,
):
    box_index = lax.axis_index(BOX)
    dir_position = lax.axis_index("dir")
    dir_index = dir_position.astype(jnp.int32).reshape(1)
    owners = lax.axis_size(BOX)
    first_box = (box_index - 1) * 8
    places = jnp.stack([dir_position, 1 - box_index % 2]).astype(jnp.int32)
    with_one = [(i, i ^ 1) for i in range(owners)]
    with_two = [(i, i + 1 - 2 * ((i + 1) % 2)) for i in range(1, owners - 1)]
    swap = [(0, 1), (1, 0)]

    half, send, leaf, mine = leaf_patterns(dir_index, sources, radiation)
    received = lax.ppermute(send, "dir", swap)
    two = lax.ppermute(half, BOX, with_two)
    one = lax.ppermute(half, BOX, with_one)
    two_swapped = lax.ppermute(two, "dir", swap)
    one_swapped = lax.ppermute(one, "dir", swap)
    mine, factors_two = lax.optimization_barrier((mine, shift2.reshape(8, 2, 64, 256)))
    level_one = level_one_patterns(dir_index, mine, received, phi_interp1, theta_interp1, shift1)

    kids = lax.all_to_all(level_one, ("xl", "z"), 0, 0, tiled=True)
    operators_two = upper_operators(il2_rel, trans2.reshape(316, 2, 128), level_one)
    leaf, near_links, operators_two = lax.optimization_barrier(
        (leaf, (near_src - first_box).astype(jnp.int32), operators_two)
    )
    leaf_two = lax.ppermute(leaf, BOX, with_two)
    leaf_one = lax.ppermute(leaf, BOX, with_one)
    near_field = near_products(near_links, places, near_blocks, sources, one, one_swapped, two, two_swapped)
    kids, near_field = lax.optimization_barrier((kids, near_field))
    terms = level_two_terms(kids, phi_interp2, theta_interp2, factors_two)

    got = lax.all_to_all(terms.reshape(128, 8, 128), ALL, 0, 0, tiled=True)
    links = link_offsets(il0_src, first_box.astype(jnp.int32).reshape(1), terms)
    operators = gather_operators(il0_rel, il0_count, trans0, links)
    leaf_incoming = leaf_translate(places, links, il0_count, operators, leaf, leaf_one, leaf_two)
    got, leaf_incoming = lax.optimization_barrier((got, leaf_incoming))
    upper = upper_translate(il2_src, got.reshape(8, 8, 2, 8, 128), operators_two)
    return near_field, leaf_incoming, upper.reshape(8, 2, 64, 1, 128)


def solution(mesh):
    fine = Mesh(mesh.devices.reshape(4, 2, 2, 4, 2), ALL)
    placed = (
        P(BOX, None, None, None),
        P(BOX, None, None, "dir", None),
        P(BOX, None),
        P(BOX, None, None, "dir"),
        P(BOX, None),
        P(BOX, None),
        P(BOX),
        P(None, None, "dir"),
        P(),
        P(),
        P(),
        P(),
        P(),
        P(),
        P(),
        P(),
        P(None, None, BOX, "dir"),
    )
    return jax.shard_map(
        local,
        mesh=fine,
        in_specs=placed,
        out_specs=(
            P(BOX, None, None, "dir"),
            P(BOX, None, None, "dir"),
            P(None, None, None, BOX, "dir"),
        ),
        check_vma=False,
    )
```
